512 devices in a mesh: section: 64 (over z_lo, y, core), tp: 8 (over x, z_hi).
Axes of the slice: x: 4, y: 8, z: 8 (z_hi: 2, z_lo: 4; z = z_hi * 4 + z_lo), core: 2. Of those that a mesh axis runs over, the one named last changes fastest.
Arguments:
- tokens: bfloat16 [2048, 6144], P('section', 'tp'), may hold values from -6 to 6
- norm_gain: float32 [6144], P('tp'), may hold values from 0.25 to 1.75
- router_weight: float32 [6144, 8], P('tp'), may hold values from -0.009765625 to 0.009765625
- routes: int32 [2048, 2], P('section'), may hold values from 0 to 7, all different within a row; in each aligned block of 32 rows (0 to 31, 32 to 63, ...) at most 12 rows name the same one
- w_gate: bfloat16 [6144, 65536], P(None, ('section', 'tp')), may hold values from -0.078125 to 0.078125
- w_up: bfloat16 [6144, 65536], P(None, ('section', 'tp')), may hold values from -0.078125 to 0.078125
- w_down: bfloat16 [65536, 6144], P('section', 'tp'), may hold values from -0.09375 to 0.09375
Outputs:
- mixed: bfloat16 [2048, 6144], P('section', 'tp')
The draws below stay inside these ranges and needn't reach their ends.
Inputs may be any that keep to these rules, and one draw needn't show every extreme that they name: `routes`: in each aligned block of 32 rows (the rows of one index of section) the two ids of a row differ, and no expert is named by more than 12 rows; some expert is named by exactly 12 rows in some block.
All inputs are finite; a program needn't handle non-finite values.
Results may differ from the reference program's by a relative error of at most 0.015.
Values may be sent and summed in bfloat16 or wider, within the bound.
No kernel may reach another device: no remote copies, remote signals or barrier semaphores. Data moves between devices by JAX's collectives and lax.ppermute only.
A program may use at most 128 MiB of HBM per device.

```python
import math
import jax
import jax.numpy as jnp
import numpy as np
from jax import lax

D = 6144
EXPERTS = 8
FF = 8192
TOP = 2
TOK_DEV = 32
CAP = 12
TOKENS = 2048
N_SECTION = 64


def steps_of(stream_key, shape, cuts, smallest, largest):
    gain = 1.0
    for dim, parts in cuts:
        draws = jax.random.uniform(jax.random.fold_in(jax.random.fold_in(stream_key, 6), dim), (parts,), jnp.float32, smallest / len(cuts), largest / len(cuts))
        gain = gain * jnp.repeat(jnp.exp(draws), shape[dim] // parts).reshape((-1,) + (1,) * (len(shape) - 1 - dim))
    return gain


def routed_block(key, own, number, rows, amount, top, bound, lean):
    order = jax.random.permutation(key, amount)
    crowded, ordinary = shares(amount, rows * top, bound, lean, True), shares(amount, rows * top, bound, lean, False)
    places = jnp.arange(amount)

    def named(tallies, turn):
        used = int((tallies > 0).sum())
        fixed = max(1, used // 4)
        moved = fixed + (places - fixed + turn * (used - fixed)) % max(1, amount - fixed)
        return jnp.zeros((amount,), jnp.int32).at[order[jnp.where(places < fixed, places, moved)]].set(jnp.asarray(tallies, jnp.int32))

    tallies = jnp.where(number % 4 == 0, named(crowded, number // 4), named(ordinary, number - number // 4 - 1))
    mixed = jax.random.permutation(jax.random.fold_in(own, 3), amount)
    source_of, receiver = mixed[0:amount // 2 * 2:2], mixed[1:amount // 2 * 2:2]
    margin = jnp.minimum(tallies[source_of] - 1, bound - tallies[receiver]) // 2
    margin = jnp.where((source_of == order[0]) | (receiver == order[0]) | (tallies[receiver] == 0), 0, jnp.maximum(margin, 0))
    moved = jax.random.randint(jax.random.fold_in(own, 4), (amount // 2,), 0, 1 << 20) % (margin + 1)
    tallies = tallies.at[source_of].add(-moved).at[receiver].add(moved)
    items = jnp.searchsorted(jnp.cumsum(tallies), jnp.arange(rows * top), side="right").astype(jnp.int32)
    table = items.reshape(top, rows).T
    table = table[jax.random.permutation(jax.random.fold_in(own, 1), rows)]
    turn = jax.random.randint(jax.random.fold_in(own, 2), (rows, 1), 0, top)
    return jnp.take_along_axis(table, (jnp.arange(top)[None, :] + turn) % top, axis=1)


def shares(number_of, total, bound, skew, full):
    portions = [(1 << 20) // math.isqrt(rank ** skew) + 1 for rank in range(1, number_of + 1)]
    largest = bound if full else min(bound, max(-(-total // number_of), total * portions[0] // sum(portions)))
    least = 1 if total - largest >= number_of - 1 else 0
    counts, rest = [largest] + [least] * (number_of - 1), total - largest - least * (number_of - 1)
    while rest > 0:
        free = [i for i in range(1, number_of) if counts[i] < largest] or [i for i in range(1, number_of) if counts[i] < bound]
        mass, budget = sum([portions[i] for i in free]), rest
        for i in free:
            addition = min(bound - counts[i], max(1, budget * portions[i] // mass), rest)
            counts[i] = counts[i] + addition
            rest = rest - addition
    return np.array(counts)


def normal_values(key, extent, width, limit, cuts=(), kind=jnp.bfloat16):
    level = steps_of(key, extent, cuts, -0.22, 0.18) if cuts else 1.0
    drawn = jax.random.normal(key, extent, jnp.float32) * width * level
    return jnp.minimum(jnp.maximum(drawn, -limit), limit).astype(kind)


def setup_inputs(seed: int = 0) -> dict:
    key_list = jax.random.split(jax.random.key(seed), 8)
    tokens = normal_values(key_list[0], (TOKENS, D), 1.0, 6.0, ((0, 64), (1, 8)))
    norm_gain = jnp.clip(1.0 + 0.15 * jax.random.normal(key_list[1], (D,), jnp.float32), 0.25, 1.75)
    router_weight = normal_values(key_list[2], (D, EXPERTS), (64 * D) ** -0.5, 0.009765625, ((0, 8),), jnp.float32)
    routes_keys = jax.random.split(jax.random.fold_in(key_list[3], 1), TOKENS // TOK_DEV)
    routes_turns = jax.random.permutation(jax.random.fold_in(key_list[3], 3), TOKENS // TOK_DEV)
    routes = jax.vmap(lambda own, number: routed_block(jax.random.fold_in(key_list[3], 2), own, number, TOK_DEV, EXPERTS, TOP, CAP, 1))(routes_keys, routes_turns).reshape((TOKENS, TOP))
    w_gate = normal_values(key_list[4], (D, EXPERTS * FF), D ** -0.5, 0.078125, ((1, 512),))
    w_up = normal_values(key_list[5], (D, EXPERTS * FF), D ** -0.5, 0.078125, ((1, 512),))
    w_down = normal_values(key_list[6], (EXPERTS * FF, D), (FF // 2) ** -0.5, 0.09375, ((0, 64), (1, 8)))
    return {"tokens": tokens, "norm_gain": norm_gain, "router_weight": router_weight, "routes": routes, "w_gate": w_gate, "w_up": w_up, "w_down": w_down}


epsilon = 1e-05

def placement_matrix(block_routes, experts, capacity):
    flat_ids = block_routes.reshape(-1).astype(jnp.int32)
    onehot = (flat_ids[:, None] == jnp.arange(experts, dtype=jnp.int32)[None, :]).astype(jnp.int32)
    ranking = lax.optimization_barrier(jnp.sum((jnp.cumsum(onehot, 0) - onehot) * onehot, 1))
    position = flat_ids * capacity + ranking
    return position[None, :] == jnp.arange(experts * capacity, dtype=jnp.int32)[:, None]

def route_probs(logits, routes, experts):
    onehot = (routes[:, :, None] == jnp.arange(experts, dtype=jnp.int32)[None, None, :]).astype(jnp.float32)
    chosen = lax.optimization_barrier(jnp.sum(onehot * logits[:, None, :], -1))
    first = jax.nn.sigmoid(chosen[:, 0] - chosen[:, 1])
    second = jax.nn.sigmoid(chosen[:, 1] - chosen[:, 0])
    return jnp.stack([first, second], 1)

def reference(tokens, norm_gain, router_weight, routes, w_gate, w_up, w_down):
    values = tokens.astype(jnp.float32)
    inverse = lax.rsqrt(lax.optimization_barrier(jnp.mean(values * values, -1)) + epsilon)
    scaled = values * norm_gain[None, :]
    normed = (scaled * inverse[:, None]).astype(jnp.bfloat16)
    logits = jnp.dot(scaled, router_weight, precision=lax.Precision.HIGHEST) * inverse[:, None]
    probs = route_probs(logits, routes, EXPERTS)
    block_routes = routes.reshape(N_SECTION, TOK_DEV, TOP)
    block_normed = normed.reshape(N_SECTION, TOK_DEV, D)

    def pack(pair):
        block_ids, block_rows = pair
        selector = placement_matrix(block_ids, EXPERTS, CAP).astype(jnp.bfloat16)
        doubled = jnp.repeat(block_rows, TOP, axis=0)
        return jnp.dot(selector, doubled, preferred_element_type=jnp.float32).astype(jnp.bfloat16)
    buffers = lax.map(pack, (block_routes, block_normed))
    expert_in = buffers.reshape(N_SECTION, EXPERTS, CAP, D).transpose(1, 0, 2, 3).reshape(EXPERTS, N_SECTION * CAP, D)

    def run_expert(pair):
        expert_rows, index = pair
        start = (index * FF).astype(jnp.int32)
        gate_cols = lax.dynamic_slice_in_dim(w_gate, start, FF, 1)
        up_cols = lax.dynamic_slice_in_dim(w_up, start, FF, 1)
        down_rows = lax.dynamic_slice_in_dim(w_down, start, FF, 0)
        gate = jnp.dot(expert_rows, gate_cols, preferred_element_type=jnp.float32)
        upward = jnp.dot(expert_rows, up_cols, preferred_element_type=jnp.float32)
        hidden = (jax.nn.silu(gate) * upward).astype(jnp.bfloat16)
        return jnp.dot(hidden, down_rows, preferred_element_type=jnp.float32)
    expert_out = lax.map(run_expert, (expert_in, jnp.arange(EXPERTS, dtype=jnp.int32)))
    per_source = expert_out.reshape(EXPERTS, N_SECTION, CAP, D).transpose(1, 0, 2, 3).reshape(N_SECTION, EXPERTS * CAP, D)
    block_probs = probs.reshape(N_SECTION, TOK_DEV * TOP)

    def combine(triple):
        block_ids, block_weights, block_out = triple
        selector = placement_matrix(block_ids, EXPERTS, CAP).astype(jnp.float32)
        weights = (selector.T * block_weights[:, None]).reshape(TOK_DEV, TOP, EXPERTS * CAP).sum(1)
        return jnp.dot(weights, block_out, precision=lax.Precision.HIGHEST)
    combined = lax.map(combine, (block_routes, block_probs, per_source)).reshape(TOKENS, D)
    return (values + combined).astype(jnp.bfloat16)
```

```python
import jax
import jax.numpy as jnp
from jax import lax
from jax.sharding import Mesh, PartitionSpec as P

D = 6144
TOP = 2
CAP = 12
HALVES = 2

epsilon = 1e-05

NAMES = ("zlo", "yh", "yl", "core", "x", "zhi")
SIZES = (4, 2, 4, 2, 4, 2)
HOMES = ("zlo", "yh", "yl")
DISPATCH = ("zlo", "yh", "yl", "zhi")


def shift(value, axis, by):
    size = lax.axis_size(axis)
    return lax.ppermute(value, axis, [(i, (i + by) % size) for i in range(size)])


def slot_ids(block_routes, experts):
    flat_ids = block_routes.reshape(-1)
    onehot = (flat_ids[:, None] == jnp.arange(experts, dtype=jnp.int32)[None, :]).astype(jnp.int32)
    ranking = jnp.sum((jnp.cumsum(onehot, 0) - onehot) * onehot, 1)
    return flat_ids * CAP + ranking


def route_probs(logits, routes, experts):
    onehot = (routes[:, :, None] == jnp.arange(experts, dtype=jnp.int32)[None, None, :]).astype(
        jnp.float32
    )
    chosen = jnp.sum(onehot * logits[:, None, :], -1)
    first = jax.nn.sigmoid(chosen[:, 0] - chosen[:, 1])
    second = jax.nn.sigmoid(chosen[:, 1] - chosen[:, 0])
    return jnp.stack([first, second], 1)


def split_sum(values):
    high = values.astype(jnp.bfloat16)
    low = (values - high.astype(jnp.float32)).astype(jnp.bfloat16)
    return high, low


def shards(tokens, norm_gain, router_weight, routes, w_gate, w_up, w_down):
    experts = router_weight.shape[1]
    count, width = tokens.shape
    units = w_gate.shape[1]
    half = width // HALVES
    nx, nz = lax.axis_size("x"), lax.axis_size("zhi")
    x, zhi = lax.axis_index("x"), lax.axis_index("zhi")
    homes = lax.axis_size("zlo") * lax.axis_size("yh") * lax.axis_size("yl")
    rows_n = homes * CAP

    wcat = jnp.concatenate([w_gate, w_up], 1).reshape(nx, nz * width, 2 * units)

    def piece(k):
        return lax.dynamic_index_in_dim(wcat, (x + k) % nx, 0, keepdims=False)

    steps = (2, 1, 3)
    w_x = {k: shift(piece(k), "x", k) for k in steps}
    w_x[0] = piece(0)
    w_c = {k: shift(w_x[k], "core", 1) for k in (0, 1, 3, 2)}

    wd = w_down.reshape(nx, nz, units, width)
    wd_ord = jnp.concatenate(
        [
            lax.dynamic_index_in_dim(
                lax.dynamic_index_in_dim(wd, (x + nx - k) % nx, 0, keepdims=False),
                (zhi + dz) % nz, 0, keepdims=False,
            )
            for dz in range(nz)
            for k in range(nx)
        ],
        0,
    )
    wd_all = jnp.concatenate([wd_ord, shift(wd_ord, "core", 1)], 0)

    gain_other = shift(norm_gain, "zhi", 1)
    gains = jnp.where(
        zhi == 0,
        jnp.concatenate([norm_gain, gain_other]),
        jnp.concatenate([gain_other, norm_gain]),
    )

    position = slot_ids(routes, experts).reshape(count, TOP)
    slots = jnp.arange(experts * CAP, dtype=jnp.int32)
    picks = (position[:, :, None] == slots[None, None, :]).astype(jnp.float32)
    chosen = picks.sum(1)
    sel = chosen.T.reshape(experts, 1, CAP, 1, count)
    eye = jnp.eye(HALVES, dtype=jnp.float32).reshape(1, HALVES, 1, HALVES, 1)
    sel2 = (sel * eye).reshape(experts * HALVES * CAP, HALVES * count).astype(jnp.bfloat16)
    tok2 = jnp.concatenate([tokens[:, :half], tokens[:, half:]], 0)
    packed = jnp.dot(sel2, tok2, preferred_element_type=jnp.float32).astype(jnp.bfloat16)
    fan = lax.axis_size("yl") * nz
    outgoing = jnp.broadcast_to(
        packed.reshape(experts, 1, HALVES * CAP, half), (experts, fan, HALVES * CAP, half)
    ).reshape(experts * fan, HALVES * CAP, half)
    arrived = lax.all_to_all(outgoing, DISPATCH, 0, 0, tiled=True)
    raw = (
        arrived.reshape(homes, nz, HALVES, CAP, half)
        .transpose(0, 3, 1, 2, 4)
        .reshape(rows_n, nz * width)
        .astype(jnp.float32)
    )
    scaled_rows = (raw * gains[None, :]).astype(jnp.bfloat16)
    squares = jnp.sum(raw * raw, 1)
    sq_hi, sq_lo = split_sum(squares)
    cols = 2 * units
    tail = jnp.concatenate([sq_hi, sq_lo]).reshape(-1, cols)
    tail_n = tail.shape[0]
    tail = jnp.pad(tail, ((0, 16 - tail_n), (0, 0)))

    def partial(k):
        own = jnp.dot(scaled_rows, w_x[k], preferred_element_type=jnp.float32)
        other = jnp.dot(scaled_rows, w_c[k], preferred_element_type=jnp.float32)
        return jnp.concatenate([own.astype(jnp.bfloat16), other.astype(jnp.bfloat16), tail], 0)

    got = [shift(partial(k), "x", -k) for k in steps] + [partial(0)]
    total = sum(g.astype(jnp.float32) for g in got)
    tail_sum = total[2 * rows_n : 2 * rows_n + tail_n].reshape(2, rows_n)
    inverse = lax.rsqrt((tail_sum[0] + tail_sum[1]) / D + epsilon)
    both = total[: 2 * rows_n].reshape(2, rows_n, cols) * inverse[None, :, None]
    hidden = (jax.nn.silu(both[..., :units]) * both[..., units:]).astype(jnp.bfloat16)

    hid_other = shift(hidden, "zhi", 1)
    gathered = []
    for h in (hidden, hid_other):
        gathered += [h] + [shift(h, "x", k) for k in (1, 2, 3)]
    wide = jnp.concatenate([g[0] for g in gathered] + [g[1] for g in gathered], 1)
    part = jnp.dot(wide, wd_all, preferred_element_type=jnp.float32).astype(jnp.bfloat16)
    back = (
        part.reshape(homes, CAP, HALVES, half)
        .transpose(0, 2, 1, 3)
        .reshape(homes, HALVES * CAP, half)
    )
    returned = lax.all_to_all(back, HOMES, 0, 0, tiled=True).reshape(homes * HALVES * CAP, half)

    values = tokens.astype(jnp.float32)
    scaled = values * norm_gain[None, :]
    router_part = jnp.concatenate(
        [
            jnp.dot(scaled, router_weight, precision=lax.Precision.HIGHEST),
            jnp.sum(values * values, -1, keepdims=True),
        ],
        1,
    )
    summed = router_part + shift(router_part, "zhi", 1)
    for by in (1, 2):
        pairs = [(i, i ^ by) for i in range(nx)]
        summed = summed + lax.ppermute(summed, "x", pairs)
    logits = summed[:, :experts] * lax.rsqrt(summed[:, experts:] / D + epsilon)
    probs = route_probs(logits, routes, experts)
    weights = (picks * probs[:, :, None]).sum(1)
    spread = jnp.broadcast_to(
        weights.reshape(1, count, experts, 1, 1, CAP)
        * jnp.eye(HALVES, dtype=jnp.float32).reshape(HALVES, 1, 1, 1, HALVES, 1),
        (HALVES, count, experts, homes // experts, HALVES, CAP),
    ).reshape(HALVES * count, homes * HALVES * CAP)
    w_hi, w_lo = split_sum(spread)
    mixed = jnp.dot(w_hi, returned, preferred_element_type=jnp.float32) + jnp.dot(
        w_lo, returned, preferred_element_type=jnp.float32
    )
    combined = jnp.concatenate([mixed[:count], mixed[count:]], 1)
    return (values + combined).astype(jnp.bfloat16)


def solution(mesh):
    fine = Mesh(mesh.devices.reshape(SIZES), NAMES)
    section, tp = NAMES[:4], NAMES[4:]
    placed = (
        P(section, tp),
        P(tp),
        P(tp, None),
        P(section, None),
        P(None, section + tp),
        P(None, section + tp),
        P(section, tp),
    )
    return jax.shard_map(
        shards, mesh=fine, in_specs=placed, out_specs=P(section, tp), check_vma=False
    )
```

```python
import functools

import jax
import jax.numpy as jnp
from jax import lax
from jax.experimental import pallas as pl
from jax.experimental.pallas import tpu as pltpu
from jax.sharding import Mesh, PartitionSpec as P

D = 6144
CAP = 12
MAIN = 8
REST = CAP - MAIN
TAIL = 16

epsilon = 1e-05

NAMES = ("zlo", "yh", "yl", "core", "x", "zhi")
SIZES = (4, 2, 4, 2, 4, 2)
HOMES = ("zlo", "yh", "yl")
DISPATCH = ("zhi", "zlo", "yh", "yl")
F32, BF16 = jnp.float32, jnp.bfloat16
VMEM_LIMIT = 48 * 1024 * 1024


def shift(value, axis, by):
    size = lax.axis_size(axis)
    return lax.ppermute(value, axis, [(i, (i + by) % size) for i in range(size)])


def local_kernel(body, out, *args, flops=0, scratch=(), smem=0):
    outs = out if isinstance(out, (list, tuple)) else [out]
    moved = sum(a.size * a.dtype.itemsize for a in args) + sum(
        o.size * o.dtype.itemsize for o in outs
    )
    return pl.pallas_call(
        body,
        out_shape=out,
        in_specs=[
            pl.BlockSpec(memory_space=pltpu.SMEM if i < smem else pltpu.VMEM)
            for i in range(len(args))
        ],
        scratch_shapes=list(scratch),
        out_specs=jax.tree.map(lambda _: pl.BlockSpec(memory_space=pltpu.VMEM), out),
        compiler_params=pltpu.CompilerParams(vmem_limit_bytes=VMEM_LIMIT),
        cost_estimate=pl.CostEstimate(flops=flops, bytes_accessed=moved, transcendentals=0),
    )(*args)


def iota(shape, dim):
    return lax.broadcasted_iota(jnp.int32, shape, dim)


def dot(a, b):
    return jnp.dot(a, b, preferred_element_type=F32)


def rest_pick(homes, half, wide):
    halves, plain = 2 * REST * homes, REST * homes
    shape = (halves, plain) if wide else (plain, halves)
    a, b = iota(shape, 0 if wide else 1), iota(shape, 1 if wide else 0)
    same = (a // (2 * REST) == b // REST) & (a % REST == b % REST)
    return (same & (a % (2 * REST) // REST == half)).astype(F32).astype(BF16)


def pack_kernel(fan, routes_ref, tok_ref, out_ref):
    count, width = tok_ref.shape
    half = width // 2
    first, second = routes_ref[0:1, :], routes_ref[1:2, :]
    experts = out_ref.shape[0] // (fan[0] * fan[1] * MAIN)
    n = experts * MAIN
    row = iota((n, count), 0)
    named = ((first == row // MAIN) | (second == row // MAIN)).astype(F32)
    earlier = (iota((count, count), 0) < iota((count, count), 1)).astype(F32).astype(BF16)
    slot = dot(named.astype(BF16), earlier)
    place = (row % MAIN).astype(F32)
    pick_main = jnp.where(slot == place, named, 0.0).astype(BF16)
    rest_place = (MAIN + row % REST).astype(F32)
    pick_rest = jnp.where(slot == rest_place, named, 0.0).astype(BF16)
    tok = tok_ref[...]
    main = dot(pick_main, tok).astype(BF16)
    rest = dot(pick_rest, tok)
    is_first = iota((n, half), 0) % MAIN < REST
    rest = jnp.where(is_first, rest[:, :half], rest[:, half:]).astype(BF16)
    for e in range(experts):
        block = slice(e * MAIN, (e + 1) * MAIN)
        main_e = jnp.concatenate([main[block]] * fan[1], 0)
        rest_e = jnp.concatenate([rest[block]] * fan[1], 0)
        for z in range(fan[0]):
            at = pl.ds((z * experts + e) * fan[1] * MAIN, fan[1] * MAIN)
            out_ref[at, :width] = main_e
            out_ref[at, width:] = rest_e


def unpack_kernel(homes, in_ref, gain_ref, rows_ref, tail_ref):
    width = gain_ref.shape[1]
    half = width // 2
    n_main, n_rest = homes * MAIN, homes * REST
    squares_main = jnp.zeros((n_main, 1), F32)
    squares_rest = jnp.zeros((n_rest, 1), F32)
    picks = [rest_pick(homes, h, False) for h in range(2)]
    for z in range(2):
        block = pl.ds(z * n_main, n_main)
        gain = gain_ref[z : z + 1, :]
        main = in_ref[block, :width].astype(F32)
        rows_ref[:n_main, z * width : (z + 1) * width] = (main * gain).astype(BF16)
        squares_main += jnp.sum(main * main, 1, keepdims=True)
        halves = in_ref[block, width:]
        for h in range(2):
            rest = dot(picks[h], halves)
            at = slice(z * width + h * half, z * width + (h + 1) * half)
            rows_ref[n_main:, at] = (rest * gain[:, h * half : (h + 1) * half]).astype(BF16)
            squares_rest += jnp.sum(rest * rest, 1, keepdims=True)

    def lanes(column):
        n = column.shape[0]
        return jnp.sum(jnp.where(iota((n, n), 0) == iota((n, n), 1), column, 0.0), 0, keepdims=True)

    a = lanes(squares_main)
    b = lanes(squares_rest)
    b = jnp.concatenate([b, jnp.zeros((1, n_main - n_rest), F32)], 1)
    row = iota((TAIL, n_main), 0)
    a_hi, b_hi = a.astype(BF16).astype(F32), b.astype(BF16).astype(F32)
    tail = jnp.where(row == 0, a_hi, jnp.where(row == 1, a - a_hi, 0.0))
    tail = jnp.where(row == 2, b_hi, jnp.where(row == 3, b - b_hi, tail))
    tail_ref[...] = tail.astype(BF16)


def partial_kernel(rows_ref, own_ref, other_ref, tail_ref, out_ref):
    n = rows_ref.shape[0]
    out_ref[:n, :] = dot(rows_ref[...], own_ref[...]).astype(BF16)
    out_ref[n : 2 * n, :] = dot(rows_ref[...], other_ref[...]).astype(BF16)
    out_ref[2 * n :, :] = tail_ref[...]


def hidden_kernel(n_main, *refs):
    out_ref = refs[-1]
    units = out_ref.shape[1]
    n = out_ref.shape[0] // 2
    tail = sum(r[2 * n :, :].astype(F32) for r in refs[:-1])
    mean_main = tail[0:1, :] + tail[1:2, :]
    mean_rest = (tail[2:3, :] + tail[3:4, :])[:, : n - n_main]

    def column(line):
        m = line.shape[1]
        return jnp.sum(jnp.where(iota((m, m), 0) == iota((m, m), 1), line, 0.0), 1, keepdims=True)

    squares = jnp.concatenate([column(mean_main), column(mean_rest)], 0)
    inverse = lax.rsqrt(squares / D + epsilon)
    for c in range(2):
        at = pl.ds(c * n, n)
        total = sum(r[at, :].astype(F32) for r in refs[:-1])
        gate, upward = total[:, :units] * inverse, total[:, units:] * inverse
        out_ref[at, :] = (jax.nn.silu(gate) * upward).astype(BF16)


def down_kernel(homes, nx, nz, at_ref, own_ref, other_ref, *refs):
    pieces, out_ref, wide_ref = refs[:-2], refs[-2], refs[-1]
    width = own_ref.shape[1]
    half = width // 2
    units = pieces[0].shape[1]
    n = homes * CAP
    n_main = homes * MAIN
    total = None
    for c, w_ref in enumerate((own_ref, other_ref)):
        for dz in range(nz):
            for k in range(nx):
                t = (at_ref[0] + nx - k) % nx * nz + (at_ref[1] + dz) % nz
                cols = pl.ds(pl.multiple_of(t * units, units), units)
                wide_ref[c, :, cols] = pieces[dz * nx + k][c * n : (c + 1) * n, :]
        term = dot(wide_ref[c], w_ref[...])
        total = term if total is None else total + term
    part = total.astype(BF16)
    out_ref[:, :width] = part[:n_main]
    rest = part[n_main:]
    out_ref[:, width:] = (
        dot(rest_pick(homes, 0, True), rest[:, :half])
        + dot(rest_pick(homes, 1, True), rest[:, half:])
    ).astype(BF16)


def route_weights(logits, routes, experts, homes):
    ids = jnp.arange(experts, dtype=jnp.int32)
    named = (routes[:, :, None] == ids[None, None, :]).astype(F32)
    chosen = jnp.sum(named * logits[:, None, :], -1)
    probs = jnp.stack(
        [
            jax.nn.sigmoid(chosen[:, 0] - chosen[:, 1]),
            jax.nn.sigmoid(chosen[:, 1] - chosen[:, 0]),
        ],
        1,
    )
    count = routes.shape[0]
    both = named.sum(1)
    slot = jnp.cumsum(both, 0) - both
    weight = (named * probs[:, :, None]).sum(1)
    place = jnp.arange(MAIN, dtype=F32)
    shape = (count, experts, homes // experts, MAIN)
    main = jnp.where(slot[:, :, None] == place, weight[:, :, None], 0.0)[:, :, None, :]
    rest_slot = MAIN + place % REST
    rest = jnp.where(slot[:, :, None] == rest_slot, weight[:, :, None], 0.0)[:, :, None, :]
    out = [jnp.broadcast_to(main, shape).reshape(count, -1)]
    for h in range(2):
        mine = (place >= REST) == (h == 1)
        out.append(jnp.broadcast_to(jnp.where(mine, rest, 0.0), shape).reshape(count, -1))
    stacked = jnp.concatenate(out, 0)
    high = stacked.astype(BF16)
    low = (stacked - high.astype(F32)).astype(BF16)
    return high, low


def combine_kernel(tok_ref, hi_ref, lo_ref, back_ref, out_ref):
    count, width = tok_ref.shape
    half = width // 2
    main = back_ref[:, :width]
    rest = back_ref[:, width:]
    at = slice(0, count)
    total = tok_ref[...].astype(F32) + dot(hi_ref[at, :], main) + dot(lo_ref[at, :], main)
    for h in range(2):
        at = slice((h + 1) * count, (h + 2) * count)
        cols = slice(h * half, (h + 1) * half)
        extra = dot(hi_ref[at, :], rest) + dot(lo_ref[at, :], rest)
        out_ref[:, cols] = (total[:, cols] + extra).astype(BF16)


def shards(tokens, norm_gain, router_weight, routes, w_gate, w_up, w_down):
    experts = router_weight.shape[1]
    count, width = tokens.shape
    units = w_gate.shape[1]
    half = width // 2
    span = width + half
    nx, nz, ny = lax.axis_size("x"), lax.axis_size("zhi"), lax.axis_size("yl")
    x, zhi = lax.axis_index("x"), lax.axis_index("zhi")
    homes = experts * ny
    n = homes * CAP
    cols = 2 * units

    def piece(k):
        at = ((x + k) % nx) * (nz * width)
        return jnp.concatenate(
            [lax.dynamic_slice_in_dim(w, at, nz * width, 0) for w in (w_gate, w_up)], 1
        )

    outgoing = local_kernel(
        functools.partial(pack_kernel, (nz, ny)),
        jax.ShapeDtypeStruct((nz * homes * MAIN, span), BF16),
        routes.T,
        tokens,
    )
    outgoing, w_gate, w_up, w_down, norm_gain = lax.optimization_barrier(
        (outgoing, w_gate, w_up, w_down, norm_gain)
    )
    arrived = lax.all_to_all(
        outgoing.reshape(nz * homes, MAIN, span), DISPATCH, 0, 0, tiled=True
    ).reshape(nz * homes * MAIN, span)

    w_x = {k: shift(piece(k), "x", k) for k in (1, 3, 2)}
    w_x[0] = piece(0)
    w_c = {k: shift(w_x[k], "core", 1) for k in (0, 1, 3, 2)}

    wd_other = shift(w_down, "core", 1)

    values = tokens.astype(F32)
    router_part = jnp.concatenate(
        [
            jnp.dot(values * norm_gain[None, :], router_weight, precision=lax.Precision.HIGHEST),
            jnp.sum(values * values, -1, keepdims=True),
        ],
        1,
    )
    summed = router_part + shift(router_part, "zhi", 1)
    for by in (1, 2):
        summed = summed + lax.ppermute(summed, "x", [(i, i ^ by) for i in range(nx)])
    logits = summed[:, :experts] * lax.rsqrt(summed[:, experts:] / D + epsilon)
    w_hi, w_lo = route_weights(logits, routes, experts, homes)

    gain_other = shift(norm_gain, "zhi", 1)
    gains = jnp.where(
        zhi == 0,
        jnp.stack([norm_gain, gain_other]),
        jnp.stack([gain_other, norm_gain]),
    )
    rows, tail = local_kernel(
        functools.partial(unpack_kernel, homes),
        [
            jax.ShapeDtypeStruct((n, nz * width), BF16),
            jax.ShapeDtypeStruct((TAIL, homes * MAIN), BF16),
        ],
        arrived,
        gains,
    )

    def partial(k):
        return local_kernel(
            partial_kernel,
            jax.ShapeDtypeStruct((2 * n + TAIL, cols), BF16),
            rows,
            w_x[k],
            w_c[k],
            tail,
            flops=4 * n * nz * width * cols,
        )

    got = [shift(partial(k), "x", -k) for k in (1, 3, 2)] + [partial(0)]
    hidden = local_kernel(
        functools.partial(hidden_kernel, homes * MAIN),
        jax.ShapeDtypeStruct((2 * n, units), BF16),
        *got,
    )

    gathered = []
    for h in (hidden, shift(hidden, "zhi", 1)):
        gathered += [h] + [shift(h, "x", k) for k in (1, 2, 3)]
    back = local_kernel(
        functools.partial(down_kernel, homes, nx, nz),
        jax.ShapeDtypeStruct((homes * MAIN, span), BF16),
        jnp.stack([x, zhi]).astype(jnp.int32),
        w_down,
        wd_other,
        *gathered,
        flops=4 * n * w_down.size,
        scratch=[pltpu.VMEM((2, n, nx * nz * units), BF16)],
        smem=1,
    )
    returned = lax.all_to_all(
        back.reshape(homes, MAIN, span), HOMES, 0, 0, tiled=True
    ).reshape(homes * MAIN, span)
    return local_kernel(
        combine_kernel,
        jax.ShapeDtypeStruct((count, width), BF16),
        tokens,
        w_hi,
        w_lo,
        returned,
    )


def solution(mesh):
    fine = Mesh(mesh.devices.reshape(SIZES), NAMES)
    section, tp = NAMES[:4], NAMES[4:]
    placed = (
        P(section, tp),
        P(tp),
        P(tp, None),
        P(section, None),
        P(None, section + tp),
        P(None, section + tp),
        P(section, tp),
    )
    return jax.shard_map(
        shards, mesh=fine, in_specs=placed, out_specs=P(section, tp), check_vma=False
    )
```

```python
import functools

import jax
import jax.numpy as jnp
from jax import lax
from jax.experimental import pallas as pl
from jax.experimental.pallas import tpu as pltpu
from jax.sharding import Mesh, PartitionSpec as P

D = 6144
CAP = 12
MAIN = 8
REST = CAP - MAIN
TAIL = 16

epsilon = 1e-05

NAMES = ("zlo", "yh", "yl", "core", "x", "zhi")
SIZES = (4, 2, 4, 2, 4, 2)
HOMES = ("zlo", "yh", "yl")
DISPATCH = ("zhi", "zlo", "yh", "yl")
F32, BF16 = jnp.float32, jnp.bfloat16
VMEM_LIMIT = 16 * 1024 * 1024
WINDOW_FLOPS = 10**10
W_ORDER = (2, 1, 3)
RS_ORDER = (1, 2, 3)


def shift(value, axis, by):
    size = lax.axis_size(axis)
    return lax.ppermute(value, axis, [(i, (i + by) % size) for i in range(size)])


def local_kernel(body, out, *args, flops=0, scratch=(), smem=0, far=0, far_out=False):
    near = len(args) - smem - far
    spaces = [pltpu.SMEM] * smem + [pltpu.VMEM] * near + [pl.ANY] * far
    outs = out if isinstance(out, (list, tuple)) else [out]
    moved = sum(a.size * a.dtype.itemsize for a in args) + sum(
        o.size * o.dtype.itemsize for o in outs
    )
    return pl.pallas_call(
        body,
        out_shape=out,
        in_specs=[pl.BlockSpec(memory_space=space) for space in spaces],
        scratch_shapes=list(scratch),
        out_specs=jax.tree.map(
            lambda _: pl.BlockSpec(memory_space=pl.ANY if far_out else pltpu.VMEM), out
        ),
        compiler_params=pltpu.CompilerParams(vmem_limit_bytes=VMEM_LIMIT),
        cost_estimate=pl.CostEstimate(flops=flops, bytes_accessed=moved, transcendentals=0),
    )(*args)


def iota(shape, dim):
    return lax.broadcasted_iota(jnp.int32, shape, dim)


def dot(a, b):
    return jnp.dot(a, b, preferred_element_type=F32)


def rest_pick(homes, half, wide):
    halves, plain = 2 * REST * homes, REST * homes
    shape = (halves, plain) if wide else (plain, halves)
    a, b = iota(shape, 0 if wide else 1), iota(shape, 1 if wide else 0)
    same = (a // (2 * REST) == b // REST) & (a % REST == b % REST)
    return (same & (a % (2 * REST) // REST == half)).astype(F32).astype(BF16)


def pack_kernel(fan, routes_ref, tok_ref, out_ref):
    count, width = tok_ref.shape
    half = width // 2
    first, second = routes_ref[0:1, :], routes_ref[1:2, :]
    experts = out_ref.shape[0] // (fan[0] * fan[1] * MAIN)
    n = experts * MAIN
    row = iota((n, count), 0)
    named = ((first == row // MAIN) | (second == row // MAIN)).astype(F32)
    earlier = (iota((count, count), 0) < iota((count, count), 1)).astype(F32).astype(BF16)
    slot = dot(named.astype(BF16), earlier)
    place = (row % MAIN).astype(F32)
    pick_main = jnp.where(slot == place, named, 0.0).astype(BF16)
    rest_place = (MAIN + row % REST).astype(F32)
    pick_rest = jnp.where(slot == rest_place, named, 0.0).astype(BF16)
    tok = tok_ref[...]
    main = dot(pick_main, tok).astype(BF16)
    rest = dot(pick_rest, tok)
    is_first = iota((n, half), 0) % MAIN < REST
    rest = jnp.where(is_first, rest[:, :half], rest[:, half:]).astype(BF16)
    for e in range(experts):
        block = slice(e * MAIN, (e + 1) * MAIN)
        main_e = jnp.concatenate([main[block]] * fan[1], 0)
        rest_e = jnp.concatenate([rest[block]] * fan[1], 0)
        for z in range(fan[0]):
            at = pl.ds((z * experts + e) * fan[1] * MAIN, fan[1] * MAIN)
            out_ref[at, :width] = main_e
            out_ref[at, width:] = rest_e


def unpack_kernel(homes, in_ref, gain_ref, rows_ref, tail_ref):
    width = gain_ref.shape[1]
    half = width // 2
    n_main, n_rest = homes * MAIN, homes * REST
    squares_main = jnp.zeros((n_main, 1), F32)
    squares_rest = jnp.zeros((n_rest, 1), F32)
    picks = [rest_pick(homes, h, False) for h in range(2)]
    for z in range(2):
        block = pl.ds(z * n_main, n_main)
        gain = gain_ref[z : z + 1, :]
        main = in_ref[block, :width].astype(F32)
        rows_ref[:n_main, z * width : (z + 1) * width] = (main * gain).astype(BF16)
        squares_main += jnp.sum(main * main, 1, keepdims=True)
        halves = in_ref[block, width:]
        for h in range(2):
            rest = dot(picks[h], halves)
            at = slice(z * width + h * half, z * width + (h + 1) * half)
            rows_ref[n_main:, at] = (rest * gain[:, h * half : (h + 1) * half]).astype(BF16)
            squares_rest += jnp.sum(rest * rest, 1, keepdims=True)

    def lanes(column):
        n = column.shape[0]
        return jnp.sum(jnp.where(iota((n, n), 0) == iota((n, n), 1), column, 0.0), 0, keepdims=True)

    a = lanes(squares_main)
    b = lanes(squares_rest)
    b = jnp.concatenate([b, jnp.zeros((1, n_main - n_rest), F32)], 1)
    row = iota((TAIL, n_main), 0)
    a_hi, b_hi = a.astype(BF16).astype(F32), b.astype(BF16).astype(F32)
    tail = jnp.where(row == 0, a_hi, jnp.where(row == 1, a - a_hi, 0.0))
    tail = jnp.where(row == 2, b_hi, jnp.where(row == 3, b - b_hi, tail))
    tail_ref[...] = tail.astype(BF16)


def partial_kernel(rows_ref, tail_ref, router_ref, own_ref, other_ref, out_ref, held_ref, sems):
    n = rows_ref.shape[0]
    copies = [
        pltpu.make_async_copy(w, held_ref.at[i], sems.at[i])
        for i, w in enumerate((own_ref, other_ref))
    ]
    for copy in copies:
        copy.start()
    for i, copy in enumerate(copies):
        copy.wait()
        out_ref[i * n : (i + 1) * n, :] = dot(rows_ref[...], held_ref[i]).astype(BF16)
    out_ref[2 * n : 2 * n + TAIL, :] = tail_ref[...]
    out_ref[2 * n + TAIL :, :] = router_ref[...]


def hidden_kernel(n_main, *refs):
    parts, out_ref = refs[:-1], refs[-1]
    units = out_ref.shape[1]
    n = (out_ref.shape[0] - 2 * TAIL) // 2
    router = sum(r[2 * n + TAIL :, :].astype(F32) for r in parts)
    router = router[:, :units] + router[:, units:]
    high = router.astype(BF16)
    out_ref[2 * n : 2 * n + TAIL, :] = high
    out_ref[2 * n + TAIL :, :] = (router - high.astype(F32)).astype(BF16)
    tail = sum(r[2 * n : 2 * n + TAIL, :].astype(F32) for r in parts)
    mean_main = tail[0:1, :] + tail[1:2, :]
    mean_rest = (tail[2:3, :] + tail[3:4, :])[:, : n - n_main]

    def column(line):
        m = line.shape[1]
        return jnp.sum(jnp.where(iota((m, m), 0) == iota((m, m), 1), line, 0.0), 1, keepdims=True)

    squares = jnp.concatenate([column(mean_main), column(mean_rest)], 0)
    inverse = lax.rsqrt(squares / D + epsilon)
    for c in range(2):
        at = pl.ds(c * n, n)
        total = sum(r[at, :].astype(F32) for r in parts)
        gate, upward = total[:, :units] * inverse, total[:, units:] * inverse
        out_ref[at, :] = (jax.nn.silu(gate) * upward).astype(BF16)


def place_hidden(at_ref, dz, nx, nz, pieces, wide_ref):
    units = pieces[0].shape[1]
    for k, piece in enumerate(pieces):
        where = (at_ref[0] + nx - k) % nx
        cols = pl.ds(pl.multiple_of(where * units, units), units)
        wide_ref[:, cols] = piece[: wide_ref.shape[0], :]


def down_part(side, homes, nx, nz, pieces, own_ref, other_ref, wide_ref):
    n = homes * CAP
    units = pieces[0].shape[1]
    total = None
    for c, w_ref in enumerate((own_ref, other_ref)):
        for x in range(nx):
            at = pl.multiple_of((x * nz + side) * units, units)
            term = dot(
                wide_ref[c * n : (c + 1) * n, x * units : (x + 1) * units],
                w_ref[pl.ds(at, units), :],
            )
            total = term if total is None else total + term
    return total


def down_first_kernel(homes, nx, nz, at_ref, own_ref, other_ref, *refs):
    pieces, out_ref, wide_ref = refs[:-2], refs[-2], refs[-1]
    place_hidden(at_ref, 0, nx, nz, pieces, wide_ref)
    out_ref[...] = down_part(at_ref[1], homes, nx, nz, pieces, own_ref, other_ref, wide_ref)


def down_last_kernel(homes, nx, nz, at_ref, own_ref, other_ref, first_ref, *refs):
    pieces, out_ref, wide_ref = refs[:-2], refs[-2], refs[-1]
    width = own_ref.shape[1]
    half = width // 2
    n_main = homes * MAIN
    place_hidden(at_ref, 1, nx, nz, pieces, wide_ref)
    total = down_part(1 - at_ref[1], homes, nx, nz, pieces, own_ref, other_ref, wide_ref)
    part = (first_ref[...] + total).astype(BF16)
    out_ref[:, :width] = part[:n_main]
    rest = part[n_main:]
    out_ref[:, width:] = (
        dot(rest_pick(homes, 0, True), rest[:, :half])
        + dot(rest_pick(homes, 1, True), rest[:, half:])
    ).astype(BF16)


def router_kernel(side_ref, tok_ref, gain_ref, gain_other_ref, router_ref, out_ref, gains_ref):
    values = tok_ref[...].astype(F32)
    count = values.shape[0]
    experts = router_ref.shape[0]
    sums = lax.dot_general(
        router_ref[...],
        values * gain_ref[...],
        (((1,), (1,)), ((), ())),
        precision=lax.Precision.HIGHEST,
        preferred_element_type=F32,
    )
    squares = jnp.sum(values * values, 1, keepdims=True)
    diagonal = iota((count, count), 0) == iota((count, count), 1)
    line = jnp.sum(jnp.where(diagonal, squares, 0.0), 0, keepdims=True)
    block = jnp.concatenate([sums, jnp.broadcast_to(line, (TAIL - experts, count))], 0)
    high = block.astype(BF16)
    low = (block - high.astype(F32)).astype(BF16)
    lanes = out_ref.shape[1] // 2
    blank = jnp.zeros((TAIL, lanes - count), BF16)
    out_ref[...] = jnp.concatenate([high, blank, low, blank], 1)
    mine = iota(gains_ref.shape, 0) == side_ref[0]
    gains_ref[...] = jnp.where(mine, gain_ref[...], gain_other_ref[...])


def weights_kernel(experts, routes_ref, own_ref, other_ref, out_ref):
    count = routes_ref.shape[1]
    rows = out_ref.shape[0] // 2 // 3
    sums = jnp.zeros((TAIL, count), F32)
    for ref in (own_ref, other_ref):
        n = ref.shape[0]
        for at in (n - 2 * TAIL, n - TAIL):
            sums += ref[at : at + TAIL, :count].astype(F32)
    logits = sums[:experts] * lax.rsqrt(sums[experts : experts + 1] / D + epsilon)
    first, second = routes_ref[0:1, :], routes_ref[1:2, :]
    ids = iota((experts, count), 0)
    one = jnp.sum(jnp.where(ids == first, logits, 0.0), 0, keepdims=True)
    two = jnp.sum(jnp.where(ids == second, logits, 0.0), 0, keepdims=True)
    p_one, p_two = jax.nn.sigmoid(one - two), jax.nn.sigmoid(two - one)
    row = iota((rows, count), 0)
    expert = row // (rows // experts)
    named = ((first == expert) | (second == expert)).astype(F32)
    earlier = (iota((count, count), 0) < iota((count, count), 1)).astype(F32).astype(BF16)
    slot = dot(named.astype(BF16), earlier)
    weight = jnp.where(first == expert, p_one, 0.0) + jnp.where(second == expert, p_two, 0.0)
    place = row % MAIN
    main = jnp.where(slot == place.astype(F32), weight, 0.0)
    rest = jnp.where(slot == (MAIN + place % REST).astype(F32), weight, 0.0)
    blocks = [main, jnp.where(place < REST, rest, 0.0), jnp.where(place >= REST, rest, 0.0)]
    for i, block in enumerate(blocks):
        high = block.astype(BF16)
        low = (block - high.astype(F32)).astype(BF16)
        out_ref[i * rows : (i + 1) * rows, :] = high
        out_ref[(3 + i) * rows : (4 + i) * rows, :] = low


def combine_kernel(tok_ref, weight_ref, back_ref, out_ref):
    width = tok_ref.shape[1]
    half = width // 2
    rows = back_ref.shape[0]

    def mix(block, part):
        total = 0.0
        for i in (block, 3 + block):
            total += lax.dot_general(
                weight_ref[i * rows : (i + 1) * rows, :],
                part,
                (((0,), (0,)), ((), ())),
                preferred_element_type=F32,
            )
        return total

    total = tok_ref[...].astype(F32) + mix(0, back_ref[:, :width])
    rest = back_ref[:, width:]
    for h in range(2):
        cols = slice(h * half, (h + 1) * half)
        out_ref[:, cols] = (total[:, cols] + mix(1 + h, rest)).astype(BF16)


def shards(tokens, norm_gain, router_weight, routes, w_gate, w_up, w_down):
    experts = router_weight.shape[1]
    count, width = tokens.shape
    units = w_gate.shape[1]
    half = width // 2
    span = width + half
    nx, nz, ny = lax.axis_size("x"), lax.axis_size("zhi"), lax.axis_size("yl")
    x, zhi = lax.axis_index("x"), lax.axis_index("zhi")
    homes = experts * ny
    n = homes * CAP
    cols = 2 * units

    def piece(k):
        at = ((x + k) % nx) * (nz * width)
        return jnp.concatenate(
            [lax.dynamic_slice_in_dim(w, at, nz * width, 0) for w in (w_gate, w_up)], 1
        )

    outgoing = local_kernel(
        functools.partial(pack_kernel, (nz, ny)),
        jax.ShapeDtypeStruct((nz * homes * MAIN, span), BF16),
        routes.T,
        tokens,
    )
    outgoing, w_gate, w_up, norm_gain = lax.optimization_barrier(
        (outgoing, w_gate, w_up, norm_gain)
    )
    arrived = lax.all_to_all(
        outgoing.reshape(nz * homes, MAIN, span), DISPATCH, 0, 0, tiled=True
    ).reshape(nz * homes * MAIN, span)

    w_x = {k: shift(piece(k), "x", k) for k in W_ORDER}
    w_x[0] = piece(0)
    w_c = {k: shift(w_x[k], "core", 1) for k in (0, 1, 3, 2)}
    wd_other = shift(w_down, "core", 1)
    router, gains = local_kernel(
        router_kernel,
        [
            jax.ShapeDtypeStruct((TAIL, cols), BF16),
            jax.ShapeDtypeStruct((nz, width), F32),
        ],
        zhi.astype(jnp.int32)[None],
        tokens,
        norm_gain[None, :],
        shift(norm_gain, "zhi", 1)[None, :],
        router_weight.T,
        flops=WINDOW_FLOPS,
        smem=1,
    )
    rows, tail = local_kernel(
        functools.partial(unpack_kernel, homes),
        [
            jax.ShapeDtypeStruct((n, nz * width), BF16),
            jax.ShapeDtypeStruct((TAIL, homes * MAIN), BF16),
        ],
        arrived,
        gains,
    )

    def partial(k):
        return local_kernel(
            partial_kernel,
            jax.ShapeDtypeStruct((2 * n + 2 * TAIL, cols), BF16),
            rows,
            tail,
            router,
            w_x[k],
            w_c[k],
            far=2,
            scratch=[
                pltpu.VMEM((2, nz * width, cols), BF16),
                pltpu.SemaphoreType.DMA((2,)),
            ],
            flops=4 * n * nz * width * cols,
        )

    got = [shift(partial(k), "x", -k) for k in RS_ORDER] + [partial(0)]
    hidden = local_kernel(
        functools.partial(hidden_kernel, homes * MAIN),
        jax.ShapeDtypeStruct((2 * n + 2 * TAIL, units), BF16),
        *got,
    )

    at = jnp.stack([x, zhi]).astype(jnp.int32)
    hid_other = shift(hidden, "zhi", 1)
    own_rows = hidden[: 2 * n]
    own_side = [own_rows] + [shift(own_rows, "x", k) for k in (1, 2, 3)]
    first = local_kernel(
        functools.partial(down_first_kernel, homes, nx, nz),
        jax.ShapeDtypeStruct((n, width), F32),
        at,
        w_down,
        wd_other,
        *own_side,
        flops=2 * n * w_down.size,
        scratch=[pltpu.VMEM((2 * n, nx * units), BF16)],
        smem=1,
    )
    other_rows = hid_other[: 2 * n]
    other_side = [other_rows] + [shift(other_rows, "x", k) for k in (1, 2, 3)]
    back = local_kernel(
        functools.partial(down_last_kernel, homes, nx, nz),
        jax.ShapeDtypeStruct((homes * MAIN, span), BF16),
        at,
        w_down,
        wd_other,
        first,
        *other_side,
        flops=2 * n * w_down.size,
        scratch=[pltpu.VMEM((2 * n, nx * units), BF16)],
        smem=1,
    )
    back, routes = lax.optimization_barrier((back, routes))
    returned = lax.all_to_all(
        back.reshape(homes, MAIN, span), HOMES, 0, 0, tiled=True
    ).reshape(homes * MAIN, span)
    weights = local_kernel(
        functools.partial(weights_kernel, experts),
        jax.ShapeDtypeStruct((6 * homes * MAIN, count), BF16),
        routes.T,
        hidden,
        hid_other,
    )
    return local_kernel(
        combine_kernel,
        jax.ShapeDtypeStruct((count, width), BF16),
        tokens,
        weights,
        returned,
    )


def solution(mesh):
    fine = Mesh(mesh.devices.reshape(SIZES), NAMES)
    section, tp = NAMES[:4], NAMES[4:]
    placed = (
        P(section, tp),
        P(tp),
        P(tp, None),
        P(section, None),
        P(None, section + tp),
        P(None, section + tp),
        P(section, tp),
    )
    return jax.shard_map(
        shards, mesh=fine, in_specs=placed, out_specs=P(section, tp), check_vma=False
    )
```

```python
import functools

import jax
import jax.numpy as jnp
from jax import lax
from jax.experimental import pallas as pl
from jax.experimental.pallas import tpu as pltpu
from jax.sharding import Mesh, PartitionSpec as P

D = 6144
CAP = 12
MAIN = 8
REST = CAP - MAIN
TAIL = 16

epsilon = 1e-05

NAMES = ("zlo", "yh", "yl", "core", "x", "zhi")
SIZES = (4, 2, 4, 2, 4, 2)
HOMES = ("zlo", "yh", "yl")
DISPATCH = ("zhi", "zlo", "yh", "yl")
F32, BF16 = jnp.float32, jnp.bfloat16
VMEM_LIMIT = 16 * 1024 * 1024
WINDOW_FLOPS = 10**11


def shift(value, axis, by):
    size = lax.axis_size(axis)
    return lax.ppermute(value, axis, [(i, (i + by) % size) for i in range(size)])


def local_kernel(body, out, *args, flops=0, scratch=(), smem=0, far=0, far_outs=(), aliases=None):
    near = len(args) - smem - far
    spaces = [pltpu.SMEM] * smem + [pltpu.VMEM] * near + [pl.ANY] * far
    outs = out if isinstance(out, (list, tuple)) else [out]
    out_specs = [
        pl.BlockSpec(memory_space=pl.ANY if i in far_outs else pltpu.VMEM)
        for i in range(len(outs))
    ]
    moved = sum(a.size * a.dtype.itemsize for a in args) + sum(
        o.size * o.dtype.itemsize for o in outs
    )
    return pl.pallas_call(
        body,
        out_shape=out,
        in_specs=[pl.BlockSpec(memory_space=space) for space in spaces],
        scratch_shapes=list(scratch),
        out_specs=out_specs if isinstance(out, list) else out_specs[0],
        input_output_aliases=aliases or {},
        compiler_params=pltpu.CompilerParams(vmem_limit_bytes=VMEM_LIMIT),
        cost_estimate=pl.CostEstimate(flops=flops, bytes_accessed=moved, transcendentals=0),
    )(*args)


def iota(shape, dim):
    return lax.broadcasted_iota(jnp.int32, shape, dim)


def dot(a, b):
    return jnp.dot(a, b, preferred_element_type=F32)


def rest_pick(homes, half, wide):
    halves, plain = 2 * REST * homes, REST * homes
    shape = (halves, plain) if wide else (plain, halves)
    a, b = iota(shape, 0 if wide else 1), iota(shape, 1 if wide else 0)
    same = (a // (2 * REST) == b // REST) & (a % REST == b % REST)
    return (same & (a % (2 * REST) // REST == half)).astype(F32).astype(BF16)


def pack_kernel(fan, routes_ref, tok_ref, out_ref):
    count, width = tok_ref.shape
    half = width // 2
    first, second = routes_ref[0:1, :], routes_ref[1:2, :]
    experts = out_ref.shape[0] // (fan[0] * fan[1] * MAIN)
    n = experts * MAIN
    row = iota((n, count), 0)
    named = ((first == row // MAIN) | (second == row // MAIN)).astype(F32)
    earlier = (iota((count, count), 0) < iota((count, count), 1)).astype(F32).astype(BF16)
    slot = dot(named.astype(BF16), earlier)
    place = (row % MAIN).astype(F32)
    pick_main = jnp.where(slot == place, named, 0.0).astype(BF16)
    rest_place = (MAIN + row % REST).astype(F32)
    pick_rest = jnp.where(slot == rest_place, named, 0.0).astype(BF16)
    tok = tok_ref[...]
    main = dot(pick_main, tok).astype(BF16)
    rest = dot(pick_rest, tok)
    is_first = iota((n, half), 0) % MAIN < REST
    rest = jnp.where(is_first, rest[:, :half], rest[:, half:]).astype(BF16)
    for e in range(experts):
        block = slice(e * MAIN, (e + 1) * MAIN)
        main_e = jnp.concatenate([main[block]] * fan[1], 0)
        rest_e = jnp.concatenate([rest[block]] * fan[1], 0)
        for z in range(fan[0]):
            at = pl.ds((z * experts + e) * fan[1] * MAIN, fan[1] * MAIN)
            out_ref[at, :width] = main_e
            out_ref[at, width:] = rest_e


def unpack_kernel(homes, in_ref, gain_ref, rows_ref, tail_ref):
    width = gain_ref.shape[1]
    half = width // 2
    n_main, n_rest = homes * MAIN, homes * REST
    squares_main = jnp.zeros((n_main, 1), F32)
    squares_rest = jnp.zeros((n_rest, 1), F32)
    picks = [rest_pick(homes, h, False) for h in range(2)]
    for z in range(2):
        block = pl.ds(z * n_main, n_main)
        gain = gain_ref[z : z + 1, :]
        main = in_ref[block, :width].astype(F32)
        rows_ref[:n_main, z * width : (z + 1) * width] = (main * gain).astype(BF16)
        squares_main += jnp.sum(main * main, 1, keepdims=True)
        halves = in_ref[block, width:]
        for h in range(2):
            rest = dot(picks[h], halves)
            at = slice(z * width + h * half, z * width + (h + 1) * half)
            rows_ref[n_main:, at] = (rest * gain[:, h * half : (h + 1) * half]).astype(BF16)
            squares_rest += jnp.sum(rest * rest, 1, keepdims=True)

    def lanes(column):
        n = column.shape[0]
        return jnp.sum(jnp.where(iota((n, n), 0) == iota((n, n), 1), column, 0.0), 0, keepdims=True)

    a = lanes(squares_main)
    b = lanes(squares_rest)
    b = jnp.concatenate([b, jnp.zeros((1, n_main - n_rest), F32)], 1)
    row = iota((TAIL, n_main), 0)
    a_hi, b_hi = a.astype(BF16).astype(F32), b.astype(BF16).astype(F32)
    tail = jnp.where(row == 0, a_hi, jnp.where(row == 1, a - a_hi, 0.0))
    tail = jnp.where(row == 2, b_hi, jnp.where(row == 3, b - b_hi, tail))
    tail_ref[...] = tail.astype(BF16)


def partial_kernel(at_ref, rows_ref, tail_ref, router_ref, *refs):
    weights, (out_ref, parts_ref, sems) = refs[:-3], refs[-3:]
    n = rows_ref.shape[0]
    block = 2 * n + 2 * TAIL
    nx = len(weights) // 2
    sent = []
    for k in range(nx):
        for c in range(2):
            part = dot(rows_ref[...], weights[2 * k + c][...])
            parts_ref[k, c * n : (c + 1) * n, :] = part.astype(BF16)
        parts_ref[k, 2 * n : 2 * n + TAIL, :] = tail_ref[...]
        parts_ref[k, 2 * n + TAIL :, :] = router_ref[...]
        to = pl.multiple_of((at_ref[0] + nx - k) % nx * block, block)
        copy = pltpu.make_async_copy(parts_ref.at[k], out_ref.at[pl.ds(to, block), :], sems.at[k])
        copy.start()
        sent.append(copy)
    for copy in sent:
        copy.wait()


def hidden_kernel(n_main, nx, in_ref, out_ref):
    units = out_ref.shape[1]
    n = (out_ref.shape[0] - 2 * TAIL) // 2
    block = 2 * n + 2 * TAIL

    def total(at, rows):
        parts = [in_ref[i * block + at : i * block + at + rows, :].astype(F32) for i in range(nx)]
        return sum(parts[1:], parts[0])

    router = total(2 * n + TAIL, TAIL)
    router = router[:, :units] + router[:, units:]
    high = router.astype(BF16)
    out_ref[2 * n : 2 * n + TAIL, :] = high
    out_ref[2 * n + TAIL :, :] = (router - high.astype(F32)).astype(BF16)
    tail = total(2 * n, TAIL)
    mean_main = tail[0:1, :] + tail[1:2, :]
    mean_rest = (tail[2:3, :] + tail[3:4, :])[:, : n - n_main]

    def column(line):
        m = line.shape[1]
        return jnp.sum(jnp.where(iota((m, m), 0) == iota((m, m), 1), line, 0.0), 1, keepdims=True)

    squares = jnp.concatenate([column(mean_main), column(mean_rest)], 0)
    inverse = lax.rsqrt(squares / D + epsilon)
    for c in range(2):
        both = total(c * n, n)
        gate, upward = both[:, :units] * inverse, both[:, units:] * inverse
        out_ref[c * n : (c + 1) * n, :] = (jax.nn.silu(gate) * upward).astype(BF16)


def down_part(at_ref, dz, n, nx, nz, pieces, own_ref, other_ref):
    units = pieces[0].shape[1]
    side = (at_ref[1] + dz) % nz
    total = None
    for c, w_ref in enumerate((own_ref, other_ref)):
        for k in range(0, nx, 2):
            wide = jnp.concatenate([p[c * n : (c + 1) * n, :] for p in pieces[k : k + 2]], 1)
            blocks = [(at_ref[0] + nx - k - i) % nx * nz + side for i in range(2)]
            w = jnp.concatenate(
                [w_ref[pl.ds(pl.multiple_of(t * units, units), units), :] for t in blocks], 0
            )
            term = dot(wide, w)
            total = term if total is None else total + term
    return total


def down_first_kernel(homes, nx, nz, at_ref, own_ref, other_ref, *refs):
    pieces, out_ref = refs[:-1], refs[-1]
    out_ref[...] = down_part(at_ref, 0, homes * CAP, nx, nz, pieces, own_ref, other_ref)


def down_last_kernel(homes, nx, nz, at_ref, own_ref, other_ref, first_ref, *refs):
    pieces, out_ref = refs[:-1], refs[-1]
    width = own_ref.shape[1]
    half = width // 2
    n_main = homes * MAIN
    total = down_part(at_ref, 1, homes * CAP, nx, nz, pieces, own_ref, other_ref)
    part = (first_ref[...] + total).astype(BF16)
    out_ref[:, :width] = part[:n_main]
    rest = part[n_main:]
    out_ref[:, width:] = (
        dot(rest_pick(homes, 0, True), rest[:, :half])
        + dot(rest_pick(homes, 1, True), rest[:, half:])
    ).astype(BF16)


def router_kernel(tok_ref, gain_ref, router_ref, _, __, out_ref, ___):
    values = tok_ref[...].astype(F32)
    count = values.shape[0]
    experts = router_ref.shape[0]
    sums = lax.dot_general(
        router_ref[...],
        values * gain_ref[...],
        (((1,), (1,)), ((), ())),
        precision=lax.Precision.HIGHEST,
        preferred_element_type=F32,
    )
    squares = jnp.sum(values * values, 1, keepdims=True)
    diagonal = iota((count, count), 0) == iota((count, count), 1)
    line = jnp.sum(jnp.where(diagonal, squares, 0.0), 0, keepdims=True)
    block = jnp.concatenate([sums, jnp.broadcast_to(line, (TAIL - experts, count))], 0)
    high = block.astype(BF16)
    low = (block - high.astype(F32)).astype(BF16)
    lanes = out_ref.shape[1] // 2
    blank = jnp.zeros((TAIL, lanes - count), BF16)
    out_ref[...] = jnp.concatenate([high, blank, low, blank], 1)


def join_kernel(in_ref, _, __, out_ref, *___):
    out_ref[...] = in_ref[...]


def gains_kernel(at_ref, gain_ref, other_ref, _, out_ref, __):
    mine = iota(out_ref.shape, 0) == at_ref[1]
    out_ref[...] = jnp.where(mine, gain_ref[...], other_ref[...])


def weights_kernel(experts, routes_ref, own_ref, other_ref, out_ref):
    count = routes_ref.shape[1]
    rows = out_ref.shape[0] // 2 // 3
    sums = jnp.zeros((TAIL, count), F32)
    for ref in (own_ref, other_ref):
        n = ref.shape[0]
        for at in (n - 2 * TAIL, n - TAIL):
            sums += ref[at : at + TAIL, :count].astype(F32)
    logits = sums[:experts] * lax.rsqrt(sums[experts : experts + 1] / D + epsilon)
    first, second = routes_ref[0:1, :], routes_ref[1:2, :]
    ids = iota((experts, count), 0)
    one = jnp.sum(jnp.where(ids == first, logits, 0.0), 0, keepdims=True)
    two = jnp.sum(jnp.where(ids == second, logits, 0.0), 0, keepdims=True)
    p_one, p_two = jax.nn.sigmoid(one - two), jax.nn.sigmoid(two - one)
    row = iota((rows, count), 0)
    expert = row // (rows // experts)
    named = ((first == expert) | (second == expert)).astype(F32)
    earlier = (iota((count, count), 0) < iota((count, count), 1)).astype(F32).astype(BF16)
    slot = dot(named.astype(BF16), earlier)
    weight = jnp.where(first == expert, p_one, 0.0) + jnp.where(second == expert, p_two, 0.0)
    place = row % MAIN
    main = jnp.where(slot == place.astype(F32), weight, 0.0)
    rest = jnp.where(slot == (MAIN + place % REST).astype(F32), weight, 0.0)
    blocks = [main, jnp.where(place < REST, rest, 0.0), jnp.where(place >= REST, rest, 0.0)]
    for i, block in enumerate(blocks):
        high = block.astype(BF16)
        low = (block - high.astype(F32)).astype(BF16)
        out_ref[i * rows : (i + 1) * rows, :] = high
        out_ref[(3 + i) * rows : (4 + i) * rows, :] = low


def combine_kernel(tok_ref, weight_ref, back_ref, out_ref):
    width = tok_ref.shape[1]
    half = width // 2
    rows = back_ref.shape[0]

    def mix(block, part):
        total = 0.0
        for i in (block, 3 + block):
            total += lax.dot_general(
                weight_ref[i * rows : (i + 1) * rows, :],
                part,
                (((0,), (0,)), ((), ())),
                preferred_element_type=F32,
            )
        return total

    total = tok_ref[...].astype(F32) + mix(0, back_ref[:, :width])
    rest = back_ref[:, width:]
    for h in range(2):
        cols = slice(h * half, (h + 1) * half)
        out_ref[:, cols] = (total[:, cols] + mix(1 + h, rest)).astype(BF16)


def shards(tokens, norm_gain, router_weight, routes, w_gate, w_up, w_down):
    experts = router_weight.shape[1]
    count, width = tokens.shape
    units = w_gate.shape[1]
    half = width // 2
    span = width + half
    nx, nz, ny = lax.axis_size("x"), lax.axis_size("zhi"), lax.axis_size("yl")
    x, zhi = lax.axis_index("x"), lax.axis_index("zhi")
    homes = experts * ny
    n = homes * CAP
    cols = 2 * units

    at = jnp.stack([x, zhi]).astype(jnp.int32)
    depth = nz * width
    piece = jax.ShapeDtypeStruct((depth, cols), BF16)

    def rows_for(k):
        start = ((x + k) % nx) * depth
        return jnp.concatenate(
            [lax.dynamic_slice_in_dim(w, start, depth, 0) for w in (w_gate, w_up)], 1
        )

    pieces = [rows_for(k) for k in range(nx)]
    w_x = {0: pieces[0], 1: shift(pieces[1], "x", 1), 3: shift(pieces[3], "x", 3)}
    outgoing = local_kernel(
        functools.partial(pack_kernel, (nz, ny)),
        jax.ShapeDtypeStruct((nz * homes * MAIN, span), BF16),
        routes.T,
        tokens,
    )
    arrived = lax.all_to_all(
        outgoing.reshape(nz * homes, MAIN, span), DISPATCH, 0, 0, tiled=True
    ).reshape(nz * homes * MAIN, span)

    router, far_piece = local_kernel(
        router_kernel,
        [jax.ShapeDtypeStruct((TAIL, cols), BF16), piece],
        tokens,
        norm_gain[None, :],
        router_weight.T,
        outgoing,
        pieces[2],
        far=2,
        far_outs=(1,),
        aliases={4: 1},
        flops=WINDOW_FLOPS,
    )
    w_x[2] = shift(far_piece, "x", 2)
    router, w_x[1], w_x[3] = local_kernel(
        join_kernel,
        [jax.ShapeDtypeStruct((TAIL, cols), BF16), piece, piece],
        router,
        w_x[1],
        w_x[3],
        far=2,
        far_outs=(1, 2),
        aliases={1: 1, 2: 2},
    )
    w_c = {k: shift(w_x[k], "core", 1) for k in (0, 1, 3)}
    wd_other = shift(w_down, "core", 1)
    gains, w_x[2] = local_kernel(
        gains_kernel,
        [jax.ShapeDtypeStruct((nz, width), F32), piece],
        at,
        norm_gain[None, :],
        shift(norm_gain, "zhi", 1)[None, :],
        w_x[2],
        smem=1,
        far=1,
        far_outs=(1,),
        aliases={3: 1},
    )
    w_c[2] = shift(w_x[2], "core", 1)
    rows, tail = local_kernel(
        functools.partial(unpack_kernel, homes),
        [
            jax.ShapeDtypeStruct((n, nz * width), BF16),
            jax.ShapeDtypeStruct((TAIL, homes * MAIN), BF16),
        ],
        arrived,
        gains,
    )

    block = 2 * n + 2 * TAIL
    parts = local_kernel(
        partial_kernel,
        [jax.ShapeDtypeStruct((nx * block, cols), BF16)],
        at,
        rows,
        tail,
        router,
        *[w[k] for k in range(nx) for w in (w_x, w_c)],
        smem=1,
        far_outs=(0,),
        flops=4 * nx * n * depth * cols,
        scratch=[pltpu.VMEM((nx, block, cols), BF16), pltpu.SemaphoreType.DMA((nx,))],
    )[0]

    def exchange(stacked):
        sent = stacked.reshape(nx, -1, stacked.shape[1])
        return lax.all_to_all(sent, "x", 0, 0, tiled=True).reshape(stacked.shape)

    hidden = local_kernel(
        functools.partial(hidden_kernel, homes * MAIN, nx),
        jax.ShapeDtypeStruct((block, units), BF16),
        exchange(parts),
    )

    hid_other = shift(hidden, "zhi", 1)
    own_rows, other_rows = hidden[: 2 * n], hid_other[: 2 * n]
    first = local_kernel(
        functools.partial(down_first_kernel, homes, nx, nz),
        jax.ShapeDtypeStruct((n, width), F32),
        at,
        w_down,
        wd_other,
        *[shift(own_rows, "x", k) if k else own_rows for k in range(nx)],
        flops=2 * n * w_down.size,
        smem=1,
    )
    back = local_kernel(
        functools.partial(down_last_kernel, homes, nx, nz),
        jax.ShapeDtypeStruct((homes * MAIN, span), BF16),
        at,
        w_down,
        wd_other,
        first,
        *[shift(other_rows, "x", k) if k else other_rows for k in range(nx)],
        flops=2 * n * w_down.size,
        smem=1,
    )
    back, routes = lax.optimization_barrier((back, routes))
    returned = lax.all_to_all(
        back.reshape(homes, MAIN, span), HOMES, 0, 0, tiled=True
    ).reshape(homes * MAIN, span)
    weights = local_kernel(
        functools.partial(weights_kernel, experts),
        jax.ShapeDtypeStruct((6 * homes * MAIN, count), BF16),
        routes.T,
        hidden,
        hid_other,
    )
    return local_kernel(
        combine_kernel,
        jax.ShapeDtypeStruct((count, width), BF16),
        tokens,
        weights,
        returned,
    )


def solution(mesh):
    fine = Mesh(mesh.devices.reshape(SIZES), NAMES)
    section, tp = NAMES[:4], NAMES[4:]
    placed = (
        P(section, tp),
        P(tp),
        P(tp, None),
        P(section, None),
        P(None, section + tp),
        P(None, section + tp),
        P(section, tp),
    )
    return jax.shard_map(
        shards, mesh=fine, in_specs=placed, out_specs=P(section, tp), check_vma=False
    )
```

```python
import functools

import jax
import jax.numpy as jnp
from jax import lax
from jax.experimental import pallas as pl
from jax.experimental.pallas import tpu as pltpu
from jax.sharding import Mesh, PartitionSpec as P

D = 6144
CAP = 12
MAIN = 8
REST = CAP - MAIN
TAIL = 16

epsilon = 1e-05

NAMES = ("zlo", "yh", "yl", "core", "x", "zhi")
SIZES = (4, 2, 4, 2, 4, 2)
HOMES = ("zlo", "yh", "yl")
DISPATCH = ("zhi", "zlo", "yh", "yl")
F32, BF16 = jnp.float32, jnp.bfloat16
VMEM_LIMIT = 16 * 1024 * 1024
WINDOW_FLOPS = 10**11


def shift(value, axis, by):
    size = lax.axis_size(axis)
    return lax.ppermute(value, axis, [(i, (i + by) % size) for i in range(size)])


def local_kernel(body, out, *args, flops=0, scratch=(), smem=0, far=0, far_outs=(), aliases=None):
    near = len(args) - smem - far
    spaces = [pltpu.SMEM] * smem + [pltpu.VMEM] * near + [pl.ANY] * far
    outs = out if isinstance(out, (list, tuple)) else [out]
    out_specs = [
        pl.BlockSpec(memory_space=pl.ANY if i in far_outs else pltpu.VMEM)
        for i in range(len(outs))
    ]
    moved = sum(a.size * a.dtype.itemsize for a in args) + sum(
        o.size * o.dtype.itemsize for o in outs
    )
    return pl.pallas_call(
        body,
        out_shape=out,
        in_specs=[pl.BlockSpec(memory_space=space) for space in spaces],
        scratch_shapes=list(scratch),
        out_specs=out_specs if isinstance(out, list) else out_specs[0],
        input_output_aliases=aliases or {},
        compiler_params=pltpu.CompilerParams(vmem_limit_bytes=VMEM_LIMIT),
        cost_estimate=pl.CostEstimate(flops=flops, bytes_accessed=moved, transcendentals=0),
    )(*args)


def iota(shape, dim):
    return lax.broadcasted_iota(jnp.int32, shape, dim)


def dot(a, b):
    return jnp.dot(a, b, preferred_element_type=F32)


def rest_pick(homes, half, wide):
    halves, plain = 2 * REST * homes, REST * homes
    shape = (halves, plain) if wide else (plain, halves)
    a, b = iota(shape, 0 if wide else 1), iota(shape, 1 if wide else 0)
    same = (a // (2 * REST) == b // REST) & (a % REST == b % REST)
    return (same & (a % (2 * REST) // REST == half)).astype(F32).astype(BF16)


def pack_kernel(fan, routes_ref, tok_ref, out_ref):
    count, width = tok_ref.shape
    half = width // 2
    first, second = routes_ref[0:1, :], routes_ref[1:2, :]
    experts = out_ref.shape[0] // (fan[0] * fan[1] * MAIN)
    n = experts * MAIN
    row = iota((n, count), 0)
    named = ((first == row // MAIN) | (second == row // MAIN)).astype(F32)
    earlier = (iota((count, count), 0) < iota((count, count), 1)).astype(F32).astype(BF16)
    slot = dot(named.astype(BF16), earlier)
    place = (row % MAIN).astype(F32)
    pick_main = jnp.where(slot == place, named, 0.0).astype(BF16)
    rest_place = (MAIN + row % REST).astype(F32)
    pick_rest = jnp.where(slot == rest_place, named, 0.0).astype(BF16)
    tok = tok_ref[...]
    main = dot(pick_main, tok).astype(BF16)
    rest = dot(pick_rest, tok)
    is_first = iota((n, half), 0) % MAIN < REST
    rest = jnp.where(is_first, rest[:, :half], rest[:, half:]).astype(BF16)
    for e in range(experts):
        block = slice(e * MAIN, (e + 1) * MAIN)
        main_e = jnp.concatenate([main[block]] * fan[1], 0)
        rest_e = jnp.concatenate([rest[block]] * fan[1], 0)
        for z in range(fan[0]):
            at = pl.ds((z * experts + e) * fan[1] * MAIN, fan[1] * MAIN)
            out_ref[at, :width] = main_e
            out_ref[at, width:] = rest_e


def unpack_kernel(homes, in_ref, gain_ref, rows_ref, tail_ref):
    width = gain_ref.shape[1]
    half = width // 2
    n_main, n_rest = homes * MAIN, homes * REST
    squares_main = jnp.zeros((n_main, 1), F32)
    squares_rest = jnp.zeros((n_rest, 1), F32)
    picks = [rest_pick(homes, h, False) for h in range(2)]
    for z in range(2):
        block = pl.ds(z * n_main, n_main)
        gain = gain_ref[z : z + 1, :]
        main = in_ref[block, :width].astype(F32)
        rows_ref[:n_main, z * width : (z + 1) * width] = (main * gain).astype(BF16)
        squares_main += jnp.sum(main * main, 1, keepdims=True)
        halves = in_ref[block, width:]
        for h in range(2):
            rest = dot(picks[h], halves)
            at = slice(z * width + h * half, z * width + (h + 1) * half)
            rows_ref[n_main:, at] = (rest * gain[:, h * half : (h + 1) * half]).astype(BF16)
            squares_rest += jnp.sum(rest * rest, 1, keepdims=True)

    def lanes(column):
        n = column.shape[0]
        return jnp.sum(jnp.where(iota((n, n), 0) == iota((n, n), 1), column, 0.0), 0, keepdims=True)

    a = lanes(squares_main)
    b = lanes(squares_rest)
    b = jnp.concatenate([b, jnp.zeros((1, n_main - n_rest), F32)], 1)
    row = iota((TAIL, n_main), 0)
    a_hi, b_hi = a.astype(BF16).astype(F32), b.astype(BF16).astype(F32)
    tail = jnp.where(row == 0, a_hi, jnp.where(row == 1, a - a_hi, 0.0))
    tail = jnp.where(row == 2, b_hi, jnp.where(row == 3, b - b_hi, tail))
    tail_ref[...] = tail.astype(BF16)


def partial_kernel(at_ref, rows_ref, tail_ref, router_ref, *refs):
    weights, (out_ref, parts_ref, sems) = refs[:-3], refs[-3:]
    n = rows_ref.shape[0]
    block = 2 * n + 2 * TAIL
    nx = len(weights) // 2
    sent = []
    for k in range(nx):
        for c in range(2):
            part = dot(rows_ref[...], weights[2 * k + c][...])
            parts_ref[k, c * n : (c + 1) * n, :] = part.astype(BF16)
        parts_ref[k, 2 * n : 2 * n + TAIL, :] = tail_ref[...]
        parts_ref[k, 2 * n + TAIL :, :] = router_ref[...]
        to = pl.multiple_of((at_ref[0] + nx - k) % nx * block, block)
        copy = pltpu.make_async_copy(parts_ref.at[k], out_ref.at[pl.ds(to, block), :], sems.at[k])
        copy.start()
        sent.append(copy)
    for copy in sent:
        copy.wait()


def hidden_kernel(n_main, nx, in_ref, out_ref):
    units = out_ref.shape[1]
    n = (out_ref.shape[0] - 2 * TAIL) // 2
    block = 2 * n + 2 * TAIL

    def total(at, rows):
        parts = [in_ref[i * block + at : i * block + at + rows, :].astype(F32) for i in range(nx)]
        return sum(parts[1:], parts[0])

    router = total(2 * n + TAIL, TAIL)
    router = router[:, :units] + router[:, units:]
    high = router.astype(BF16)
    out_ref[2 * n : 2 * n + TAIL, :] = high
    out_ref[2 * n + TAIL :, :] = (router - high.astype(F32)).astype(BF16)
    tail = total(2 * n, TAIL)
    mean_main = tail[0:1, :] + tail[1:2, :]
    mean_rest = (tail[2:3, :] + tail[3:4, :])[:, : n - n_main]

    def column(line):
        m = line.shape[1]
        return jnp.sum(jnp.where(iota((m, m), 0) == iota((m, m), 1), line, 0.0), 1, keepdims=True)

    squares = jnp.concatenate([column(mean_main), column(mean_rest)], 0)
    inverse = lax.rsqrt(squares / D + epsilon)
    for c in range(2):
        both = total(c * n, n)
        gate, upward = both[:, :units] * inverse, both[:, units:] * inverse
        out_ref[c * n : (c + 1) * n, :] = (jax.nn.silu(gate) * upward).astype(BF16)


def down_part(at_ref, dz, n, nx, nz, pieces, own_ref, other_ref):
    units = pieces[0].shape[1]
    side = (at_ref[1] + dz) % nz
    total = None
    for c, w_ref in enumerate((own_ref, other_ref)):
        for k in range(0, nx, 2):
            wide = jnp.concatenate([p[c * n : (c + 1) * n, :] for p in pieces[k : k + 2]], 1)
            blocks = [(at_ref[0] + nx - k - i) % nx * nz + side for i in range(2)]
            w = jnp.concatenate(
                [w_ref[pl.ds(pl.multiple_of(t * units, units), units), :] for t in blocks], 0
            )
            term = dot(wide, w)
            total = term if total is None else total + term
    return total


def down_first_kernel(homes, nx, nz, at_ref, own_ref, other_ref, *refs):
    pieces, out_ref = refs[:-1], refs[-1]
    out_ref[...] = down_part(at_ref, 0, homes * CAP, nx, nz, pieces, own_ref, other_ref)


def down_last_kernel(homes, nx, nz, at_ref, own_ref, other_ref, first_ref, *refs):
    pieces, out_ref = refs[:-1], refs[-1]
    width = own_ref.shape[1]
    half = width // 2
    n_main = homes * MAIN
    total = down_part(at_ref, 1, homes * CAP, nx, nz, pieces, own_ref, other_ref)
    part = (first_ref[...] + total).astype(BF16)
    out_ref[:, :width] = part[:n_main]
    rest = part[n_main:]
    out_ref[:, width:] = (
        dot(rest_pick(homes, 0, True), rest[:, :half])
        + dot(rest_pick(homes, 1, True), rest[:, half:])
    ).astype(BF16)


def router_kernel(tok_ref, gain_ref, router_ref, _, __, ___, out_ref, *passed):
    values = tok_ref[...].astype(F32)
    count = values.shape[0]
    experts = router_ref.shape[0]
    sums = lax.dot_general(
        router_ref[...],
        values * gain_ref[...],
        (((1,), (1,)), ((), ())),
        precision=lax.Precision.HIGHEST,
        preferred_element_type=F32,
    )
    squares = jnp.sum(values * values, 1, keepdims=True)
    diagonal = iota((count, count), 0) == iota((count, count), 1)
    line = jnp.sum(jnp.where(diagonal, squares, 0.0), 0, keepdims=True)
    block = jnp.concatenate([sums, jnp.broadcast_to(line, (TAIL - experts, count))], 0)
    high = block.astype(BF16)
    low = (block - high.astype(F32)).astype(BF16)
    lanes = out_ref.shape[1] // 2
    blank = jnp.zeros((TAIL, lanes - count), BF16)
    out_ref[...] = jnp.concatenate([high, blank, low, blank], 1)


def join_kernel(in_ref, _, out_ref, __):
    out_ref[...] = in_ref[...]


def gains_kernel(at_ref, gain_ref, other_ref, _, __, out_ref, *passed):
    mine = iota(out_ref.shape, 0) == at_ref[1]
    out_ref[...] = jnp.where(mine, gain_ref[...], other_ref[...])


def weights_kernel(experts, routes_ref, own_ref, other_ref, out_ref):
    count = routes_ref.shape[1]
    rows = out_ref.shape[0] // 2 // 3
    sums = jnp.zeros((TAIL, count), F32)
    for ref in (own_ref, other_ref):
        n = ref.shape[0]
        for at in (n - 2 * TAIL, n - TAIL):
            sums += ref[at : at + TAIL, :count].astype(F32)
    logits = sums[:experts] * lax.rsqrt(sums[experts : experts + 1] / D + epsilon)
    first, second = routes_ref[0:1, :], routes_ref[1:2, :]
    ids = iota((experts, count), 0)
    one = jnp.sum(jnp.where(ids == first, logits, 0.0), 0, keepdims=True)
    two = jnp.sum(jnp.where(ids == second, logits, 0.0), 0, keepdims=True)
    p_one, p_two = jax.nn.sigmoid(one - two), jax.nn.sigmoid(two - one)
    row = iota((rows, count), 0)
    expert = row // (rows // experts)
    named = ((first == expert) | (second == expert)).astype(F32)
    earlier = (iota((count, count), 0) < iota((count, count), 1)).astype(F32).astype(BF16)
    slot = dot(named.astype(BF16), earlier)
    weight = jnp.where(first == expert, p_one, 0.0) + jnp.where(second == expert, p_two, 0.0)
    place = row % MAIN
    main = jnp.where(slot == place.astype(F32), weight, 0.0)
    rest = jnp.where(slot == (MAIN + place % REST).astype(F32), weight, 0.0)
    blocks = [main, jnp.where(place < REST, rest, 0.0), jnp.where(place >= REST, rest, 0.0)]
    for i, block in enumerate(blocks):
        high = block.astype(BF16)
        low = (block - high.astype(F32)).astype(BF16)
        out_ref[i * rows : (i + 1) * rows, :] = high
        out_ref[(3 + i) * rows : (4 + i) * rows, :] = low


def combine_kernel(tok_ref, weight_ref, back_ref, out_ref):
    width = tok_ref.shape[1]
    half = width // 2
    rows = back_ref.shape[0]

    def mix(block, part):
        total = 0.0
        for i in (block, 3 + block):
            total += lax.dot_general(
                weight_ref[i * rows : (i + 1) * rows, :],
                part,
                (((0,), (0,)), ((), ())),
                preferred_element_type=F32,
            )
        return total

    total = tok_ref[...].astype(F32) + mix(0, back_ref[:, :width])
    rest = back_ref[:, width:]
    for h in range(2):
        cols = slice(h * half, (h + 1) * half)
        out_ref[:, cols] = (total[:, cols] + mix(1 + h, rest)).astype(BF16)


def shards(tokens, norm_gain, router_weight, routes, w_gate, w_up, w_down):
    experts = router_weight.shape[1]
    count, width = tokens.shape
    units = w_gate.shape[1]
    half = width // 2
    span = width + half
    nx, nz, ny = lax.axis_size("x"), lax.axis_size("zhi"), lax.axis_size("yl")
    x, zhi = lax.axis_index("x"), lax.axis_index("zhi")
    homes = experts * ny
    n = homes * CAP
    cols = 2 * units

    at = jnp.stack([x, zhi]).astype(jnp.int32)
    depth = nz * width
    piece = jax.ShapeDtypeStruct((depth, cols), BF16)

    def rows_for(k, *ws):
        start = ((x + k) % nx) * depth
        return jnp.concatenate([lax.dynamic_slice_in_dim(w, start, depth, 0) for w in ws], 1)

    w_x = {2: shift(rows_for(2, w_gate, w_up), "x", 2)}
    outgoing = local_kernel(
        functools.partial(pack_kernel, (nz, ny)),
        jax.ShapeDtypeStruct((nz * homes * MAIN, span), BF16),
        routes.T,
        tokens,
    )
    outgoing, w_gate, w_up = lax.optimization_barrier((outgoing, w_gate, w_up))
    arrived = lax.all_to_all(
        outgoing.reshape(nz * homes, MAIN, span), DISPATCH, 0, 0, tiled=True
    ).reshape(nz * homes * MAIN, span)

    router, right, left = local_kernel(
        router_kernel,
        [jax.ShapeDtypeStruct((TAIL, cols), BF16), piece, piece],
        tokens,
        norm_gain[None, :],
        router_weight.T,
        outgoing,
        rows_for(1, w_gate, w_up),
        rows_for(3, w_gate, w_up),
        far=3,
        far_outs=(1, 2),
        aliases={4: 1, 5: 2},
        flops=WINDOW_FLOPS,
    )
    w_x[0] = rows_for(0, w_gate, w_up)
    w_x[1], w_x[3] = shift(right, "x", 1), shift(left, "x", 3)
    router, w_x[2] = local_kernel(
        join_kernel,
        [jax.ShapeDtypeStruct((TAIL, cols), BF16), piece],
        router,
        w_x[2],
        far=1,
        far_outs=(1,),
        aliases={1: 1},
    )
    w_c = {k: shift(w_x[k], "core", 1) for k in (2, 0)}
    wd_other = shift(w_down, "core", 1)
    gains, w_x[1], w_x[3] = local_kernel(
        gains_kernel,
        [jax.ShapeDtypeStruct((nz, width), F32), piece, piece],
        at,
        norm_gain[None, :],
        shift(norm_gain, "zhi", 1)[None, :],
        w_x[1],
        w_x[3],
        smem=1,
        far=2,
        far_outs=(1, 2),
        aliases={3: 1, 4: 2},
    )
    w_c[1], w_c[3] = shift(w_x[1], "core", 1), shift(w_x[3], "core", 1)
    rows, tail = local_kernel(
        functools.partial(unpack_kernel, homes),
        [
            jax.ShapeDtypeStruct((n, nz * width), BF16),
            jax.ShapeDtypeStruct((TAIL, homes * MAIN), BF16),
        ],
        arrived,
        gains,
    )

    block = 2 * n + 2 * TAIL
    parts = local_kernel(
        partial_kernel,
        [jax.ShapeDtypeStruct((nx * block, cols), BF16)],
        at,
        rows,
        tail,
        router,
        *[w[k] for k in range(nx) for w in (w_x, w_c)],
        smem=1,
        far_outs=(0,),
        flops=4 * nx * n * depth * cols,
        scratch=[pltpu.VMEM((nx, block, cols), BF16), pltpu.SemaphoreType.DMA((nx,))],
    )[0]

    def exchange(stacked):
        sent = stacked.reshape(nx, -1, stacked.shape[1])
        return lax.all_to_all(sent, "x", 0, 0, tiled=True).reshape(stacked.shape)

    hidden = local_kernel(
        functools.partial(hidden_kernel, homes * MAIN, nx),
        jax.ShapeDtypeStruct((block, units), BF16),
        exchange(parts),
    )

    hid_other = shift(hidden, "zhi", 1)
    own_rows, other_rows = hidden[: 2 * n], hid_other[: 2 * n]
    first = local_kernel(
        functools.partial(down_first_kernel, homes, nx, nz),
        jax.ShapeDtypeStruct((n, width), F32),
        at,
        w_down,
        wd_other,
        *[shift(own_rows, "x", k) if k else own_rows for k in range(nx)],
        flops=2 * n * w_down.size,
        smem=1,
    )
    back = local_kernel(
        functools.partial(down_last_kernel, homes, nx, nz),
        jax.ShapeDtypeStruct((homes * MAIN, span), BF16),
        at,
        w_down,
        wd_other,
        first,
        *[shift(other_rows, "x", k) if k else other_rows for k in range(nx)],
        flops=2 * n * w_down.size,
        smem=1,
    )
    back, routes = lax.optimization_barrier((back, routes))
    returned = lax.all_to_all(
        back.reshape(homes, MAIN, span), HOMES, 0, 0, tiled=True
    ).reshape(homes * MAIN, span)
    weights = local_kernel(
        functools.partial(weights_kernel, experts),
        jax.ShapeDtypeStruct((6 * homes * MAIN, count), BF16),
        routes.T,
        hidden,
        hid_other,
    )
    return local_kernel(
        combine_kernel,
        jax.ShapeDtypeStruct((count, width), BF16),
        tokens,
        weights,
        returned,
    )


def solution(mesh):
    fine = Mesh(mesh.devices.reshape(SIZES), NAMES)
    section, tp = NAMES[:4], NAMES[4:]
    placed = (
        P(section, tp),
        P(tp),
        P(tp, None),
        P(section, None),
        P(None, section + tp),
        P(None, section + tp),
        P(section, tp),
    )
    return jax.shard_map(
        shards, mesh=fine, in_specs=placed, out_specs=P(section, tp), check_vma=False
    )
```

```python
import functools

import jax
import jax.numpy as jnp
from jax import lax
from jax.experimental import pallas as pl
from jax.experimental.pallas import tpu as pltpu
from jax.sharding import Mesh, PartitionSpec as P

D = 6144
CAP = 12
MAIN = 8
REST = CAP - MAIN
SIDE = 128
TAIL = 16

epsilon = 1e-05

NAMES = ("zlo", "yh", "yl", "core", "x", "zhi")
SIZES = (4, 2, 4, 2, 4, 2)
HOMES = ("zlo", "yh", "yl")
DISPATCH = ("zhi", "zlo", "yh", "yl")
F32, BF16 = jnp.float32, jnp.bfloat16
VMEM_LIMIT = 16 * 1024 * 1024
WINDOW_FLOPS = 10**11


def shift(value, axis, by):
    size = lax.axis_size(axis)
    return lax.ppermute(value, axis, [(i, (i + by) % size) for i in range(size)])


def local_kernel(body, out, *args, flops=0, scratch=(), smem=0, far=0, far_outs=(), aliases=None):
    near = len(args) - smem - far
    spaces = [pltpu.SMEM] * smem + [pltpu.VMEM] * near + [pl.ANY] * far
    outs = out if isinstance(out, (list, tuple)) else [out]
    out_specs = [
        pl.BlockSpec(memory_space=pl.ANY if i in far_outs else pltpu.VMEM)
        for i in range(len(outs))
    ]
    moved = sum(a.size * a.dtype.itemsize for a in args) + sum(
        o.size * o.dtype.itemsize for o in outs
    )
    return pl.pallas_call(
        body,
        out_shape=out,
        in_specs=[pl.BlockSpec(memory_space=space) for space in spaces],
        scratch_shapes=list(scratch),
        out_specs=out_specs if isinstance(out, list) else out_specs[0],
        input_output_aliases=aliases or {},
        compiler_params=pltpu.CompilerParams(vmem_limit_bytes=VMEM_LIMIT),
        cost_estimate=pl.CostEstimate(flops=flops, bytes_accessed=moved, transcendentals=0),
    )(*args)


def iota(shape, dim):
    return lax.broadcasted_iota(jnp.int32, shape, dim)


def dot(a, b):
    return jnp.dot(a, b, preferred_element_type=F32)


def rest_pick(homes, half, wide):
    halves, plain = 2 * REST * homes, REST * homes
    shape = (halves, plain) if wide else (plain, halves)
    a, b = iota(shape, 0 if wide else 1), iota(shape, 1 if wide else 0)
    same = (a // (2 * REST) == b // REST) & (a % REST == b % REST)
    return (same & (a % (2 * REST) // REST == half)).astype(F32).astype(BF16)


def split(values):
    high = values.astype(BF16)
    return high, (values - high.astype(F32)).astype(BF16)


def pack_kernel(fan, routes_ref, tok_ref, gain_ref, out_ref):
    count, width = tok_ref.shape
    half = width // 2
    span = width + half
    first, second = routes_ref[0:1, :], routes_ref[1:2, :]
    experts = out_ref.shape[0] // (fan[0] * fan[1] * MAIN)
    n = experts * MAIN
    row = iota((n, count), 0)
    named = ((first == row // MAIN) | (second == row // MAIN)).astype(F32)
    earlier = (iota((count, count), 0) < iota((count, count), 1)).astype(F32).astype(BF16)
    slot = dot(named.astype(BF16), earlier)
    place = (row % MAIN).astype(F32)
    pick_main = jnp.where(slot == place, named, 0.0).astype(BF16)
    rest_place = (MAIN + row % REST).astype(F32)
    pick_rest = jnp.where(slot == rest_place, named, 0.0).astype(BF16)
    values = tok_ref[...].astype(F32)
    tok = (values * gain_ref[...]).astype(BF16)
    high, low = split(jnp.sum(values * values, 1, keepdims=True))
    lane = iota((count, SIDE), 1)
    zero = jnp.zeros((count, SIDE), F32)
    high, low = high.astype(F32) + zero, low.astype(F32) + zero
    side = 0.0
    for pick, at in ((pick_main, 0), (pick_rest, 2)):
        lanes = jnp.where(lane == at, high, jnp.where(lane == at + 1, low, 0.0))
        side += dot(pick, lanes.astype(BF16))
    main = dot(pick_main, tok).astype(BF16)
    rest = dot(pick_rest, tok)
    is_first = iota((n, half), 0) % MAIN < REST
    rest = jnp.where(is_first, rest[:, :half], rest[:, half:]).astype(BF16)
    side = side.astype(BF16)
    for e in range(experts):
        block = slice(e * MAIN, (e + 1) * MAIN)
        parts = [jnp.concatenate([p[block]] * fan[1], 0) for p in (main, rest, side)]
        for z in range(fan[0]):
            at = pl.ds((z * experts + e) * fan[1] * MAIN, fan[1] * MAIN)
            out_ref[at, :width] = parts[0]
            out_ref[at, width:span] = parts[1]
            out_ref[at, span:] = parts[2]


def unpack_kernel(homes, width, in_ref, rows_ref, tail_ref):
    half = width // 2
    span = width + half
    n_main, n_rest = homes * MAIN, homes * REST
    squares = jnp.zeros((n_main, SIDE), F32)
    picks = [rest_pick(homes, h, False) for h in range(2)]
    for z in range(2):
        block = pl.ds(z * n_main, n_main)
        rows_ref[:n_main, z * width : (z + 1) * width] = in_ref[block, :width]
        halves = in_ref[block, width:span]
        for h in range(2):
            at = slice(z * width + h * half, z * width + (h + 1) * half)
            rows_ref[n_main:, at] = dot(picks[h], halves).astype(BF16)
        squares += in_ref[block, span:].astype(F32)
    squares_main = squares[:, 0:1] + squares[:, 1:2]
    of_first = (iota((n_main, 1), 0) % MAIN < REST).astype(F32)
    squares_rest = (squares[:, 2:3] + squares[:, 3:4]) * of_first

    def lanes(column):
        n = column.shape[0]
        return jnp.sum(jnp.where(iota((n, n), 0) == iota((n, n), 1), column, 0.0), 0, keepdims=True)

    a = lanes(squares_main)
    source, lane = iota((n_main, n_main), 0), iota((n_main, n_main), 1)
    same = (source // MAIN == lane // REST) & (source % MAIN == lane % REST) & (lane < n_rest)
    b = jnp.sum(jnp.where(same, squares_rest, 0.0), 0, keepdims=True)
    row = iota((TAIL, n_main), 0)
    a_hi, b_hi = a.astype(BF16).astype(F32), b.astype(BF16).astype(F32)
    tail = jnp.where(row == 0, a_hi, jnp.where(row == 1, a - a_hi, 0.0))
    tail = jnp.where(row == 2, b_hi, jnp.where(row == 3, b - b_hi, tail))
    tail_ref[...] = tail.astype(BF16)


def partial_kernel(rows_ref, tail_ref, router_ref, own_ref, other_ref, out_ref):
    n = rows_ref.shape[0]
    for c, w_ref in enumerate((own_ref, other_ref)):
        out_ref[c * n : (c + 1) * n, :] = dot(rows_ref[...], w_ref[...]).astype(BF16)
    out_ref[2 * n : 2 * n + TAIL, :] = tail_ref[...]
    out_ref[2 * n + TAIL :, :] = router_ref[...]


def hidden_kernel(n_main, *refs):
    out_ref = refs[-1]
    units = out_ref.shape[1]
    n = (out_ref.shape[0] - 2 * TAIL) // 2

    def total(at, rows):
        parts = [r[at : at + rows, :].astype(F32) for r in refs[:-1]]
        return sum(parts[1:], parts[0])

    router = total(2 * n + TAIL, TAIL)
    router = router[:, :units] + router[:, units:]
    high = router.astype(BF16)
    out_ref[2 * n : 2 * n + TAIL, :] = high
    out_ref[2 * n + TAIL :, :] = (router - high.astype(F32)).astype(BF16)
    tail = total(2 * n, TAIL)
    mean_main = tail[0:1, :] + tail[1:2, :]
    mean_rest = (tail[2:3, :] + tail[3:4, :])[:, : n - n_main]

    def column(line):
        m = line.shape[1]
        return jnp.sum(jnp.where(iota((m, m), 0) == iota((m, m), 1), line, 0.0), 1, keepdims=True)

    squares = jnp.concatenate([column(mean_main), column(mean_rest)], 0)
    inverse = lax.rsqrt(squares / D + epsilon)
    for c in range(2):
        both = total(c * n, n)
        gate, upward = both[:, :units] * inverse, both[:, units:] * inverse
        out_ref[c * n : (c + 1) * n, :] = (jax.nn.silu(gate) * upward).astype(BF16)


def down_part(at_ref, dz, n, nx, nz, pieces, own_ref, other_ref):
    units = pieces[0].shape[1]
    side = (at_ref[1] + dz) % nz
    total = None
    for c, w_ref in enumerate((own_ref, other_ref)):
        for k in range(0, nx, 2):
            wide = jnp.concatenate([p[c * n : (c + 1) * n, :] for p in pieces[k : k + 2]], 1)
            blocks = [(at_ref[0] + nx - k - i) % nx * nz + side for i in range(2)]
            w = jnp.concatenate(
                [w_ref[pl.ds(pl.multiple_of(t * units, units), units), :] for t in blocks], 0
            )
            term = dot(wide, w)
            total = term if total is None else total + term
    return total


def down_first_kernel(homes, nx, nz, at_ref, own_ref, other_ref, *refs):
    pieces, out_ref = refs[:-1], refs[-1]
    out_ref[...] = down_part(at_ref, 0, homes * CAP, nx, nz, pieces, own_ref, other_ref)


def down_last_kernel(homes, nx, nz, at_ref, own_ref, other_ref, first_ref, *refs):
    pieces, out_ref = refs[:-1], refs[-1]
    width = own_ref.shape[1]
    half = width // 2
    n_main = homes * MAIN
    total = down_part(at_ref, 1, homes * CAP, nx, nz, pieces, own_ref, other_ref)
    part = (first_ref[...] + total).astype(BF16)
    out_ref[:, :width] = part[:n_main]
    rest = part[n_main:]
    out_ref[:, width:] = (
        dot(rest_pick(homes, 0, True), rest[:, :half])
        + dot(rest_pick(homes, 1, True), rest[:, half:])
    ).astype(BF16)


def router_kernel(_, tok_ref, gain_ref, router_ref, *refs):
    out_ref = refs[4]
    values = tok_ref[...].astype(F32)
    count = values.shape[0]
    experts = router_ref.shape[0]
    sums = lax.dot_general(
        router_ref[...],
        values * gain_ref[...],
        (((1,), (1,)), ((), ())),
        precision=lax.Precision.HIGHEST,
        preferred_element_type=F32,
    )
    squares = jnp.sum(values * values, 1, keepdims=True)
    diagonal = iota((count, count), 0) == iota((count, count), 1)
    line = jnp.sum(jnp.where(diagonal, squares, 0.0), 0, keepdims=True)
    block = jnp.concatenate([sums, jnp.broadcast_to(line, (TAIL - experts, count))], 0)
    high = block.astype(BF16)
    low = (block - high.astype(F32)).astype(BF16)
    lanes = out_ref.shape[1] // 2
    blank = jnp.zeros((TAIL, lanes - count), BF16)
    out_ref[...] = jnp.concatenate([high, blank, low, blank], 1)


def join_kernel(in_ref, _, out_ref, __):
    out_ref[...] = in_ref[...]


def weights_kernel(experts, routes_ref, own_ref, other_ref, out_ref):
    count = routes_ref.shape[1]
    rows = out_ref.shape[0] // 2 // 3
    sums = jnp.zeros((TAIL, count), F32)
    for ref in (own_ref, other_ref):
        n = ref.shape[0]
        for at in (n - 2 * TAIL, n - TAIL):
            sums += ref[at : at + TAIL, :count].astype(F32)
    logits = sums[:experts] * lax.rsqrt(sums[experts : experts + 1] / D + epsilon)
    first, second = routes_ref[0:1, :], routes_ref[1:2, :]
    ids = iota((experts, count), 0)
    one = jnp.sum(jnp.where(ids == first, logits, 0.0), 0, keepdims=True)
    two = jnp.sum(jnp.where(ids == second, logits, 0.0), 0, keepdims=True)
    p_one, p_two = jax.nn.sigmoid(one - two), jax.nn.sigmoid(two - one)
    row = iota((rows, count), 0)
    expert = row // (rows // experts)
    named = ((first == expert) | (second == expert)).astype(F32)
    earlier = (iota((count, count), 0) < iota((count, count), 1)).astype(F32).astype(BF16)
    slot = dot(named.astype(BF16), earlier)
    weight = jnp.where(first == expert, p_one, 0.0) + jnp.where(second == expert, p_two, 0.0)
    place = row % MAIN
    main = jnp.where(slot == place.astype(F32), weight, 0.0)
    rest = jnp.where(slot == (MAIN + place % REST).astype(F32), weight, 0.0)
    blocks = [main, jnp.where(place < REST, rest, 0.0), jnp.where(place >= REST, rest, 0.0)]
    for i, block in enumerate(blocks):
        high = block.astype(BF16)
        low = (block - high.astype(F32)).astype(BF16)
        out_ref[i * rows : (i + 1) * rows, :] = high
        out_ref[(3 + i) * rows : (4 + i) * rows, :] = low


def combine_kernel(tok_ref, weight_ref, back_ref, out_ref):
    width = tok_ref.shape[1]
    half = width // 2
    rows = back_ref.shape[0]

    def mix(block, part):
        total = 0.0
        for i in (block, 3 + block):
            total += lax.dot_general(
                weight_ref[i * rows : (i + 1) * rows, :],
                part,
                (((0,), (0,)), ((), ())),
                preferred_element_type=F32,
            )
        return total

    total = tok_ref[...].astype(F32) + mix(0, back_ref[:, :width])
    rest = back_ref[:, width:]
    for h in range(2):
        cols = slice(h * half, (h + 1) * half)
        out_ref[:, cols] = (total[:, cols] + mix(1 + h, rest)).astype(BF16)


def shards(tokens, norm_gain, router_weight, routes, w_gate, w_up, w_down):
    experts = router_weight.shape[1]
    count, width = tokens.shape
    units = w_gate.shape[1]
    half = width // 2
    span = width + half
    nx, nz, ny = lax.axis_size("x"), lax.axis_size("zhi"), lax.axis_size("yl")
    x, zhi = lax.axis_index("x"), lax.axis_index("zhi")
    homes = experts * ny
    n = homes * CAP
    cols = 2 * units

    at = jnp.stack([x, zhi]).astype(jnp.int32)
    depth = nz * width
    piece = jax.ShapeDtypeStruct((depth, cols), BF16)

    def rows_for(k, *ws):
        start = ((x + k) % nx) * depth
        return jnp.concatenate([lax.dynamic_slice_in_dim(w, start, depth, 0) for w in ws], 1)

    w_x = {2: shift(rows_for(2, w_gate, w_up), "x", 2)}
    outgoing = local_kernel(
        functools.partial(pack_kernel, (nz, ny)),
        jax.ShapeDtypeStruct((nz * homes * MAIN, span + SIDE), BF16),
        routes.T,
        tokens,
        norm_gain[None, :],
    )
    outgoing, w_gate, w_up = lax.optimization_barrier((outgoing, w_gate, w_up))
    arrived = lax.all_to_all(
        outgoing.reshape(nz * homes, MAIN, span + SIDE), DISPATCH, 0, 0, tiled=True
    ).reshape(nz * homes * MAIN, span + SIDE)

    router, right, left, w_x[0] = local_kernel(
        router_kernel,
        [jax.ShapeDtypeStruct((TAIL, cols), BF16), piece, piece, piece],
        at,
        tokens,
        norm_gain[None, :],
        router_weight.T,
        outgoing,
        rows_for(1, w_gate, w_up),
        rows_for(3, w_gate, w_up),
        rows_for(0, w_gate, w_up),
        smem=1,
        far=4,
        far_outs=(1, 2, 3),
        aliases={5: 1, 6: 2, 7: 3},
        flops=WINDOW_FLOPS,
    )
    w_x[1], w_x[3] = shift(right, "x", 1), shift(left, "x", 3)
    router, w_x[2] = local_kernel(
        join_kernel,
        [jax.ShapeDtypeStruct((TAIL, cols), BF16), piece],
        router,
        w_x[2],
        far=1,
        far_outs=(1,),
        aliases={1: 1},
    )
    w_c = {k: shift(w_x[k], "core", 1) for k in (2, 0)}
    w_c[1], w_c[3] = shift(w_x[1], "core", 1), shift(w_x[3], "core", 1)
    rows, tail = local_kernel(
        functools.partial(unpack_kernel, homes, width),
        [
            jax.ShapeDtypeStruct((n, nz * width), BF16),
            jax.ShapeDtypeStruct((TAIL, homes * MAIN), BF16),
        ],
        arrived,
    )

    block = 2 * n + 2 * TAIL
    def partial(k):
        return local_kernel(
            partial_kernel,
            jax.ShapeDtypeStruct((block, cols), BF16),
            rows,
            tail,
            router,
            w_x[k],
            w_c[k],
            flops=4 * n * depth * cols,
        )

    mine = partial(0)
    got = [shift(partial(k), "x", -k) for k in (1, 3, 2)] + [mine]
    wd_other = shift(w_down, "core", 1)

    hidden = local_kernel(
        functools.partial(hidden_kernel, homes * MAIN),
        jax.ShapeDtypeStruct((block, units), BF16),
        *got,
    )

    hid_other = shift(hidden, "zhi", 1)
    own_rows, other_rows = hidden[: 2 * n], hid_other[: 2 * n]
    first = local_kernel(
        functools.partial(down_first_kernel, homes, nx, nz),
        jax.ShapeDtypeStruct((n, width), F32),
        at,
        w_down,
        wd_other,
        *[shift(own_rows, "x", k) if k else own_rows for k in range(nx)],
        flops=2 * n * w_down.size,
        smem=1,
    )
    back = local_kernel(
        functools.partial(down_last_kernel, homes, nx, nz),
        jax.ShapeDtypeStruct((homes * MAIN, span), BF16),
        at,
        w_down,
        wd_other,
        first,
        *[shift(other_rows, "x", k) if k else other_rows for k in range(nx)],
        flops=2 * n * w_down.size,
        smem=1,
    )
    back, routes = lax.optimization_barrier((back, routes))
    returned = lax.all_to_all(
        back.reshape(homes, MAIN, span), HOMES, 0, 0, tiled=True
    ).reshape(homes * MAIN, span)
    weights = local_kernel(
        functools.partial(weights_kernel, experts),
        jax.ShapeDtypeStruct((6 * homes * MAIN, count), BF16),
        routes.T,
        hidden,
        hid_other,
    )
    return local_kernel(
        combine_kernel,
        jax.ShapeDtypeStruct((count, width), BF16),
        tokens,
        weights,
        returned,
    )


def solution(mesh):
    fine = Mesh(mesh.devices.reshape(SIZES), NAMES)
    section, tp = NAMES[:4], NAMES[4:]
    placed = (
        P(section, tp),
        P(tp),
        P(tp, None),
        P(section, None),
        P(None, section + tp),
        P(None, section + tp),
        P(section, tp),
    )
    return jax.shard_map(
        shards, mesh=fine, in_specs=placed, out_specs=P(section, tp), check_vma=False
    )
```

```python
import functools

import jax
import jax.numpy as jnp
from jax import lax
from jax.experimental import pallas as pl
from jax.experimental.pallas import tpu as pltpu
from jax.sharding import Mesh, PartitionSpec as P

D = 6144
CAP = 12
MAIN = 8
REST = CAP - MAIN
SIDE = 128
TAIL = 16

epsilon = 1e-05

NAMES = ("zlo", "yh", "yl", "core", "x", "zhi")
SIZES = (4, 2, 4, 2, 4, 2)
HOMES = ("zlo", "yh", "yl")
DISPATCH = ("zhi", "zlo", "yh", "yl")
F32, BF16 = jnp.float32, jnp.bfloat16
VMEM_LIMIT = 16 * 1024 * 1024
WINDOW_FLOPS = 10**11
FIRST_FLOPS = 10**10


def shift(value, axis, by):
    size = lax.axis_size(axis)
    return lax.ppermute(value, axis, [(i, (i + by) % size) for i in range(size)])


def local_kernel(body, out, *args, flops=0, scratch=(), smem=0, far=0, far_outs=(), aliases=None):
    near = len(args) - smem - far
    spaces = [pltpu.SMEM] * smem + [pltpu.VMEM] * near + [pl.ANY] * far
    outs = out if isinstance(out, (list, tuple)) else [out]
    out_specs = [
        pl.BlockSpec(memory_space=pl.ANY if i in far_outs else pltpu.VMEM)
        for i in range(len(outs))
    ]
    moved = sum(a.size * a.dtype.itemsize for a in args) + sum(
        o.size * o.dtype.itemsize for o in outs
    )
    return pl.pallas_call(
        body,
        out_shape=out,
        in_specs=[pl.BlockSpec(memory_space=space) for space in spaces],
        scratch_shapes=list(scratch),
        out_specs=out_specs if isinstance(out, list) else out_specs[0],
        input_output_aliases=aliases or {},
        compiler_params=pltpu.CompilerParams(vmem_limit_bytes=VMEM_LIMIT),
        cost_estimate=pl.CostEstimate(flops=flops, bytes_accessed=moved, transcendentals=0),
    )(*args)


def iota(shape, dim):
    return lax.broadcasted_iota(jnp.int32, shape, dim)


def dot(a, b):
    return jnp.dot(a, b, preferred_element_type=F32)


def rest_pick(homes, half, wide):
    halves, plain = 2 * REST * homes, REST * homes
    shape = (halves, plain) if wide else (plain, halves)
    a, b = iota(shape, 0 if wide else 1), iota(shape, 1 if wide else 0)
    same = (a // (2 * REST) == b // REST) & (a % REST == b % REST)
    return (same & (a % (2 * REST) // REST == half)).astype(F32).astype(BF16)


def split(values):
    high = values.astype(BF16)
    return high, (values - high.astype(F32)).astype(BF16)


def pack_kernel(fan, routes_ref, tok_ref, gain_ref, out_ref):
    count, width = tok_ref.shape
    half = width // 2
    span = width + half
    first, second = routes_ref[0:1, :], routes_ref[1:2, :]
    experts = out_ref.shape[0] // (fan[0] * fan[1] * MAIN)
    n = experts * MAIN
    row = iota((n, count), 0)
    named = ((first == row // MAIN) | (second == row // MAIN)).astype(F32)
    earlier = (iota((count, count), 0) < iota((count, count), 1)).astype(F32).astype(BF16)
    slot = dot(named.astype(BF16), earlier)
    place = (row % MAIN).astype(F32)
    pick_main = jnp.where(slot == place, named, 0.0).astype(BF16)
    rest_place = (MAIN + row % REST).astype(F32)
    pick_rest = jnp.where(slot == rest_place, named, 0.0).astype(BF16)
    values = tok_ref[...].astype(F32)
    tok = (values * gain_ref[...]).astype(BF16)
    high, low = split(jnp.sum(values * values, 1, keepdims=True))
    lane = iota((count, SIDE), 1)
    zero = jnp.zeros((count, SIDE), F32)
    high, low = high.astype(F32) + zero, low.astype(F32) + zero
    side = 0.0
    for pick, at in ((pick_main, 0), (pick_rest, 2)):
        lanes = jnp.where(lane == at, high, jnp.where(lane == at + 1, low, 0.0))
        side += dot(pick, lanes.astype(BF16))
    main = dot(pick_main, tok).astype(BF16)
    rest = dot(pick_rest, tok)
    is_first = iota((n, half), 0) % MAIN < REST
    rest = jnp.where(is_first, rest[:, :half], rest[:, half:]).astype(BF16)
    side = side.astype(BF16)
    for e in range(experts):
        block = slice(e * MAIN, (e + 1) * MAIN)
        parts = [jnp.concatenate([p[block]] * fan[1], 0) for p in (main, rest, side)]
        for z in range(fan[0]):
            at = pl.ds((z * experts + e) * fan[1] * MAIN, fan[1] * MAIN)
            out_ref[at, :width] = parts[0]
            out_ref[at, width:span] = parts[1]
            out_ref[at, span:] = parts[2]


def unpack_kernel(homes, width, in_ref, rows_ref, tail_ref):
    half = width // 2
    span = width + half
    n_main, n_rest = homes * MAIN, homes * REST
    squares = jnp.zeros((n_main, SIDE), F32)
    picks = [rest_pick(homes, h, False) for h in range(2)]
    for z in range(2):
        block = pl.ds(z * n_main, n_main)
        rows_ref[:n_main, z * width : (z + 1) * width] = in_ref[block, :width]
        halves = in_ref[block, width:span]
        for h in range(2):
            at = slice(z * width + h * half, z * width + (h + 1) * half)
            rows_ref[n_main:, at] = dot(picks[h], halves).astype(BF16)
        squares += in_ref[block, span:].astype(F32)
    squares_main = squares[:, 0:1] + squares[:, 1:2]
    of_first = (iota((n_main, 1), 0) % MAIN < REST).astype(F32)
    squares_rest = (squares[:, 2:3] + squares[:, 3:4]) * of_first

    def lanes(column):
        n = column.shape[0]
        return jnp.sum(jnp.where(iota((n, n), 0) == iota((n, n), 1), column, 0.0), 0, keepdims=True)

    a = lanes(squares_main)
    source, lane = iota((n_main, n_main), 0), iota((n_main, n_main), 1)
    same = (source // MAIN == lane // REST) & (source % MAIN == lane % REST) & (lane < n_rest)
    b = jnp.sum(jnp.where(same, squares_rest, 0.0), 0, keepdims=True)
    row = iota((TAIL, n_main), 0)
    a_hi, b_hi = a.astype(BF16).astype(F32), b.astype(BF16).astype(F32)
    tail = jnp.where(row == 0, a_hi, jnp.where(row == 1, a - a_hi, 0.0))
    tail = jnp.where(row == 2, b_hi, jnp.where(row == 3, b - b_hi, tail))
    tail_ref[...] = tail.astype(BF16)


def partial_kernel(rows_ref, tail_ref, router_ref, own_ref, other_ref, out_ref):
    n = rows_ref.shape[0]
    for c, w_ref in enumerate((own_ref, other_ref)):
        out_ref[c * n : (c + 1) * n, :] = dot(rows_ref[...], w_ref[...]).astype(BF16)
    out_ref[2 * n : 2 * n + TAIL, :] = tail_ref[...]
    out_ref[2 * n + TAIL :, :] = router_ref[...]


def hidden_kernel(n_main, *refs):
    out_ref = refs[-1]
    units = out_ref.shape[1]
    n = (out_ref.shape[0] - 2 * TAIL) // 2

    def total(at, rows):
        parts = [r[at : at + rows, :].astype(F32) for r in refs[:-1]]
        return sum(parts[1:], parts[0])

    router = total(2 * n + TAIL, TAIL)
    router = router[:, :units] + router[:, units:]
    high = router.astype(BF16)
    out_ref[2 * n : 2 * n + TAIL, :] = high
    out_ref[2 * n + TAIL :, :] = (router - high.astype(F32)).astype(BF16)
    tail = total(2 * n, TAIL)
    mean_main = tail[0:1, :] + tail[1:2, :]
    mean_rest = (tail[2:3, :] + tail[3:4, :])[:, : n - n_main]

    def column(line):
        m = line.shape[1]
        return jnp.sum(jnp.where(iota((m, m), 0) == iota((m, m), 1), line, 0.0), 1, keepdims=True)

    squares = jnp.concatenate([column(mean_main), column(mean_rest)], 0)
    inverse = lax.rsqrt(squares / D + epsilon)
    for c in range(2):
        both = total(c * n, n)
        gate, upward = both[:, :units] * inverse, both[:, units:] * inverse
        out_ref[c * n : (c + 1) * n, :] = (jax.nn.silu(gate) * upward).astype(BF16)


def repeat_kernel(in_ref, out_ref):
    n = in_ref.shape[0] - 2 * TAIL
    for i in range(out_ref.shape[0] // n):
        out_ref[i * n : (i + 1) * n, :] = in_ref[:n, :]


def down_part(at_ref, dz, n, nx, nz, pieces, own_ref, other_ref):
    units = pieces[0].shape[1]
    side = (at_ref[1] + dz) % nz
    total = None
    for c, w_ref in enumerate((own_ref, other_ref)):
        for k in range(0, nx, 2):
            wide = jnp.concatenate([p[c * n : (c + 1) * n, :] for p in pieces[k : k + 2]], 1)
            blocks = [(at_ref[0] + nx - k - i) % nx * nz + side for i in range(2)]
            w = jnp.concatenate(
                [w_ref[pl.ds(pl.multiple_of(t * units, units), units), :] for t in blocks], 0
            )
            term = dot(wide, w)
            total = term if total is None else total + term
    return total


def down_first_kernel(homes, nx, nz, at_ref, own_ref, other_ref, *refs):
    pieces, out_ref, rest_ref = refs[:-2], refs[-2], refs[-1]
    units = pieces[0].shape[1]
    for c, w_ref in enumerate((own_ref, other_ref)):
        for x in range(nx):
            t = x * nz + (at_ref[1] + 1) % nz
            rest_ref[(c * nx + x) * units : (c * nx + x + 1) * units, :] = w_ref[
                pl.ds(pl.multiple_of(t * units, units), units), :
            ]
    out_ref[...] = down_part(at_ref, 0, homes * CAP, nx, nz, pieces, own_ref, other_ref)


def down_last_kernel(homes, nx, first_ref, rest_ref, hid_ref, out_ref):
    width = first_ref.shape[1]
    half = width // 2
    n, n_main = homes * CAP, homes * MAIN
    depth = rest_ref.shape[0] // 2
    total = first_ref[...]
    for c in range(2):
        starts = [(2 * x + c) * n for x in range(nx)]
        wide = jnp.concatenate([hid_ref[at : at + n, :] for at in starts], 1)
        total += dot(wide, rest_ref[c * depth : (c + 1) * depth, :])
    part = total.astype(BF16)
    out_ref[:, :width] = part[:n_main]
    rest = part[n_main:]
    out_ref[:, width:] = (
        dot(rest_pick(homes, 0, True), rest[:, :half])
        + dot(rest_pick(homes, 1, True), rest[:, half:])
    ).astype(BF16)


def router_kernel(_, tok_ref, gain_ref, router_ref, *refs):
    out_ref = refs[4]
    values = tok_ref[...].astype(F32)
    count = values.shape[0]
    experts = router_ref.shape[0]
    sums = lax.dot_general(
        router_ref[...],
        values * gain_ref[...],
        (((1,), (1,)), ((), ())),
        precision=lax.Precision.HIGHEST,
        preferred_element_type=F32,
    )
    squares = jnp.sum(values * values, 1, keepdims=True)
    diagonal = iota((count, count), 0) == iota((count, count), 1)
    line = jnp.sum(jnp.where(diagonal, squares, 0.0), 0, keepdims=True)
    block = jnp.concatenate([sums, jnp.broadcast_to(line, (TAIL - experts, count))], 0)
    high = block.astype(BF16)
    low = (block - high.astype(F32)).astype(BF16)
    lanes = out_ref.shape[1] // 2
    blank = jnp.zeros((TAIL, lanes - count), BF16)
    out_ref[...] = jnp.concatenate([high, blank, low, blank], 1)


def join_kernel(in_ref, _, out_ref, __):
    out_ref[...] = in_ref[...]


def weights_kernel(experts, routes_ref, own_ref, other_ref, out_ref):
    count = routes_ref.shape[1]
    rows = out_ref.shape[0] // 2 // 3
    sums = jnp.zeros((TAIL, count), F32)
    for ref in (own_ref, other_ref):
        n = ref.shape[0]
        for at in (n - 2 * TAIL, n - TAIL):
            sums += ref[at : at + TAIL, :count].astype(F32)
    logits = sums[:experts] * lax.rsqrt(sums[experts : experts + 1] / D + epsilon)
    first, second = routes_ref[0:1, :], routes_ref[1:2, :]
    ids = iota((experts, count), 0)
    one = jnp.sum(jnp.where(ids == first, logits, 0.0), 0, keepdims=True)
    two = jnp.sum(jnp.where(ids == second, logits, 0.0), 0, keepdims=True)
    p_one, p_two = jax.nn.sigmoid(one - two), jax.nn.sigmoid(two - one)
    row = iota((rows, count), 0)
    expert = row // (rows // experts)
    named = ((first == expert) | (second == expert)).astype(F32)
    earlier = (iota((count, count), 0) < iota((count, count), 1)).astype(F32).astype(BF16)
    slot = dot(named.astype(BF16), earlier)
    weight = jnp.where(first == expert, p_one, 0.0) + jnp.where(second == expert, p_two, 0.0)
    place = row % MAIN
    main = jnp.where(slot == place.astype(F32), weight, 0.0)
    rest = jnp.where(slot == (MAIN + place % REST).astype(F32), weight, 0.0)
    blocks = [main, jnp.where(place < REST, rest, 0.0), jnp.where(place >= REST, rest, 0.0)]
    for i, block in enumerate(blocks):
        high = block.astype(BF16)
        low = (block - high.astype(F32)).astype(BF16)
        out_ref[i * rows : (i + 1) * rows, :] = high
        out_ref[(3 + i) * rows : (4 + i) * rows, :] = low


def combine_kernel(tok_ref, weight_ref, back_ref, out_ref):
    width = tok_ref.shape[1]
    half = width // 2
    rows = back_ref.shape[0]

    def mix(block, part):
        total = 0.0
        for i in (block, 3 + block):
            total += lax.dot_general(
                weight_ref[i * rows : (i + 1) * rows, :],
                part,
                (((0,), (0,)), ((), ())),
                preferred_element_type=F32,
            )
        return total

    total = tok_ref[...].astype(F32) + mix(0, back_ref[:, :width])
    rest = back_ref[:, width:]
    for h in range(2):
        cols = slice(h * half, (h + 1) * half)
        out_ref[:, cols] = (total[:, cols] + mix(1 + h, rest)).astype(BF16)


def shards(tokens, norm_gain, router_weight, routes, w_gate, w_up, w_down):
    experts = router_weight.shape[1]
    count, width = tokens.shape
    units = w_gate.shape[1]
    half = width // 2
    span = width + half
    nx, nz, ny = lax.axis_size("x"), lax.axis_size("zhi"), lax.axis_size("yl")
    x, zhi = lax.axis_index("x"), lax.axis_index("zhi")
    homes = experts * ny
    n = homes * CAP
    cols = 2 * units

    at = jnp.stack([x, zhi]).astype(jnp.int32)
    depth = nz * width
    piece = jax.ShapeDtypeStruct((depth, cols), BF16)

    def rows_for(k, *ws):
        start = ((x + k) % nx) * depth
        return jnp.concatenate([lax.dynamic_slice_in_dim(w, start, depth, 0) for w in ws], 1)

    w_x = {2: shift(rows_for(2, w_gate, w_up), "x", 2)}
    outgoing = local_kernel(
        functools.partial(pack_kernel, (nz, ny)),
        jax.ShapeDtypeStruct((nz * homes * MAIN, span + SIDE), BF16),
        routes.T,
        tokens,
        norm_gain[None, :],
    )
    outgoing, w_gate, w_up = lax.optimization_barrier((outgoing, w_gate, w_up))
    arrived = lax.all_to_all(
        outgoing.reshape(nz * homes, MAIN, span + SIDE), DISPATCH, 0, 0, tiled=True
    ).reshape(nz * homes * MAIN, span + SIDE)

    router, right, left, w_x[0] = local_kernel(
        router_kernel,
        [jax.ShapeDtypeStruct((TAIL, cols), BF16), piece, piece, piece],
        at,
        tokens,
        norm_gain[None, :],
        router_weight.T,
        outgoing,
        rows_for(1, w_gate, w_up),
        rows_for(3, w_gate, w_up),
        rows_for(0, w_gate, w_up),
        smem=1,
        far=4,
        far_outs=(1, 2, 3),
        aliases={5: 1, 6: 2, 7: 3},
        flops=WINDOW_FLOPS,
    )
    w_x[1], w_x[3] = shift(right, "x", 1), shift(left, "x", 3)
    router, w_x[2] = local_kernel(
        join_kernel,
        [jax.ShapeDtypeStruct((TAIL, cols), BF16), piece],
        router,
        w_x[2],
        far=1,
        far_outs=(1,),
        aliases={1: 1},
    )
    w_c = {k: shift(w_x[k], "core", 1) for k in (2, 0)}
    w_c[1], w_c[3] = shift(w_x[1], "core", 1), shift(w_x[3], "core", 1)
    rows, tail = local_kernel(
        functools.partial(unpack_kernel, homes, width),
        [
            jax.ShapeDtypeStruct((n, nz * width), BF16),
            jax.ShapeDtypeStruct((TAIL, homes * MAIN), BF16),
        ],
        arrived,
    )

    block = 2 * n + 2 * TAIL
    def partial(k):
        return local_kernel(
            partial_kernel,
            jax.ShapeDtypeStruct((block, cols), BF16),
            rows,
            tail,
            router,
            w_x[k],
            w_c[k],
            flops=4 * n * depth * cols,
        )

    mine = partial(0)
    got = [shift(partial(k), "x", -k) for k in (1, 3, 2)] + [mine]
    wd_other = shift(w_down, "core", 1)

    hidden = local_kernel(
        functools.partial(hidden_kernel, homes * MAIN),
        jax.ShapeDtypeStruct((block, units), BF16),
        *got,
    )

    hid_other = shift(hidden, "zhi", 1)
    own_rows = hidden[: 2 * n]
    other_rows = local_kernel(
        repeat_kernel, jax.ShapeDtypeStruct((nx * 2 * n, units), BF16), hid_other
    )
    other_rows = lax.all_to_all(
        other_rows.reshape(nx, 2 * n, units), "x", 0, 0, tiled=True
    ).reshape(nx * 2 * n, units)
    first, w_rest = local_kernel(
        functools.partial(down_first_kernel, homes, nx, nz),
        [
            jax.ShapeDtypeStruct((n, width), F32),
            jax.ShapeDtypeStruct((2 * nx * units, width), BF16),
        ],
        at,
        w_down,
        wd_other,
        *[shift(own_rows, "x", k) if k else own_rows for k in range(nx)],
        flops=FIRST_FLOPS,
        smem=1,
    )
    back = local_kernel(
        functools.partial(down_last_kernel, homes, nx),
        jax.ShapeDtypeStruct((homes * MAIN, span), BF16),
        first,
        w_rest,
        other_rows,
        flops=2 * n * w_down.size,
    )
    back, routes = lax.optimization_barrier((back, routes))
    returned = lax.all_to_all(
        back.reshape(homes, MAIN, span), HOMES, 0, 0, tiled=True
    ).reshape(homes * MAIN, span)
    weights = local_kernel(
        functools.partial(weights_kernel, experts),
        jax.ShapeDtypeStruct((6 * homes * MAIN, count), BF16),
        routes.T,
        hidden,
        hid_other,
    )
    return local_kernel(
        combine_kernel,
        jax.ShapeDtypeStruct((count, width), BF16),
        tokens,
        weights,
        returned,
    )


def solution(mesh):
    fine = Mesh(mesh.devices.reshape(SIZES), NAMES)
    section, tp = NAMES[:4], NAMES[4:]
    placed = (
        P(section, tp),
        P(tp),
        P(tp, None),
        P(section, None),
        P(None, section + tp),
        P(None, section + tp),
        P(section, tp),
    )
    return jax.shard_map(
        shards, mesh=fine, in_specs=placed, out_specs=P(section, tp), check_vma=False
    )
```

```python
import functools

import jax
import jax.numpy as jnp
from jax import lax
from jax.experimental import pallas as pl
from jax.experimental.pallas import tpu as pltpu
from jax.sharding import Mesh, PartitionSpec as P

D = 6144
CAP = 12
MAIN = 8
REST = CAP - MAIN
SIDE = 128
TAIL = 16

epsilon = 1e-05

NAMES = ("zlo", "yh", "yl", "core", "x", "zhi")
SIZES = (4, 2, 4, 2, 4, 2)
HOMES = ("zlo", "yh", "yl")
DISPATCH = ("zhi", "zlo", "yh", "yl")
F32, BF16 = jnp.float32, jnp.bfloat16
VMEM_LIMIT = 16 * 1024 * 1024
WINDOW_FLOPS = 10**11
FIRST_FLOPS = 10**10


def shift(value, axis, by):
    size = lax.axis_size(axis)
    return lax.ppermute(value, axis, [(i, (i + by) % size) for i in range(size)])


def local_kernel(body, out, *args, flops=0, scratch=(), smem=0, far=0, far_outs=(), aliases=None):
    near = len(args) - smem - far
    spaces = [pltpu.SMEM] * smem + [pltpu.VMEM] * near + [pl.ANY] * far
    outs = out if isinstance(out, (list, tuple)) else [out]
    out_specs = [
        pl.BlockSpec(memory_space=pl.ANY if i in far_outs else pltpu.VMEM)
        for i in range(len(outs))
    ]
    moved = sum(a.size * a.dtype.itemsize for a in args) + sum(
        o.size * o.dtype.itemsize for o in outs
    )
    return pl.pallas_call(
        body,
        out_shape=out,
        in_specs=[pl.BlockSpec(memory_space=space) for space in spaces],
        scratch_shapes=list(scratch),
        out_specs=out_specs if isinstance(out, list) else out_specs[0],
        input_output_aliases=aliases or {},
        compiler_params=pltpu.CompilerParams(vmem_limit_bytes=VMEM_LIMIT),
        cost_estimate=pl.CostEstimate(flops=flops, bytes_accessed=moved, transcendentals=0),
    )(*args)


def iota(shape, dim):
    return lax.broadcasted_iota(jnp.int32, shape, dim)


def dot(a, b):
    return jnp.dot(a, b, preferred_element_type=F32)


def rest_pick(homes, half, wide):
    halves, plain = 2 * REST * homes, REST * homes
    shape = (halves, plain) if wide else (plain, halves)
    a, b = iota(shape, 0 if wide else 1), iota(shape, 1 if wide else 0)
    same = (a // (2 * REST) == b // REST) & (a % REST == b % REST)
    return (same & (a % (2 * REST) // REST == half)).astype(F32).astype(BF16)


def split(values):
    high = values.astype(BF16)
    return high, (values - high.astype(F32)).astype(BF16)


def pack_kernel(fan, routes_ref, tok_ref, gain_ref, out_ref):
    count, width = tok_ref.shape
    half = width // 2
    span = width + half
    first, second = routes_ref[0:1, :], routes_ref[1:2, :]
    experts = out_ref.shape[0] // (fan[0] * fan[1] * MAIN)
    n = experts * MAIN
    row = iota((n, count), 0)
    named = ((first == row // MAIN) | (second == row // MAIN)).astype(F32)
    earlier = (iota((count, count), 0) < iota((count, count), 1)).astype(F32).astype(BF16)
    slot = dot(named.astype(BF16), earlier)
    place = (row % MAIN).astype(F32)
    pick_main = jnp.where(slot == place, named, 0.0).astype(BF16)
    rest_place = (MAIN + row % REST).astype(F32)
    pick_rest = jnp.where(slot == rest_place, named, 0.0).astype(BF16)
    values = tok_ref[...].astype(F32)
    tok = (values * gain_ref[...]).astype(BF16)
    high, low = split(jnp.sum(values * values, 1, keepdims=True))
    lane = iota((count, SIDE), 1)
    zero = jnp.zeros((count, SIDE), F32)
    high, low = high.astype(F32) + zero, low.astype(F32) + zero
    side = 0.0
    for pick, at in ((pick_main, 0), (pick_rest, 2)):
        lanes = jnp.where(lane == at, high, jnp.where(lane == at + 1, low, 0.0))
        side += dot(pick, lanes.astype(BF16))
    main = dot(pick_main, tok).astype(BF16)
    rest = dot(pick_rest, tok)
    is_first = iota((n, half), 0) % MAIN < REST
    rest = jnp.where(is_first, rest[:, :half], rest[:, half:]).astype(BF16)
    side = side.astype(BF16)
    for e in range(experts):
        block = slice(e * MAIN, (e + 1) * MAIN)
        parts = [jnp.concatenate([p[block]] * fan[1], 0) for p in (main, rest, side)]
        for z in range(fan[0]):
            at = pl.ds((z * experts + e) * fan[1] * MAIN, fan[1] * MAIN)
            out_ref[at, :width] = parts[0]
            out_ref[at, width:span] = parts[1]
            out_ref[at, span:] = parts[2]


def unpack_kernel(homes, width, in_ref, rows_ref, tail_ref):
    half = width // 2
    span = width + half
    n_main, n_rest = homes * MAIN, homes * REST
    squares = jnp.zeros((n_main, SIDE), F32)
    picks = [rest_pick(homes, h, False) for h in range(2)]
    for z in range(2):
        block = pl.ds(z * n_main, n_main)
        rows_ref[:n_main, z * width : (z + 1) * width] = in_ref[block, :width]
        halves = in_ref[block, width:span]
        for h in range(2):
            at = slice(z * width + h * half, z * width + (h + 1) * half)
            rows_ref[n_main:, at] = dot(picks[h], halves).astype(BF16)
        squares += in_ref[block, span:].astype(F32)
    squares_main = squares[:, 0:1] + squares[:, 1:2]
    of_first = (iota((n_main, 1), 0) % MAIN < REST).astype(F32)
    squares_rest = (squares[:, 2:3] + squares[:, 3:4]) * of_first

    def lanes(column):
        n = column.shape[0]
        return jnp.sum(jnp.where(iota((n, n), 0) == iota((n, n), 1), column, 0.0), 0, keepdims=True)

    a = lanes(squares_main)
    source, lane = iota((n_main, n_main), 0), iota((n_main, n_main), 1)
    same = (source // MAIN == lane // REST) & (source % MAIN == lane % REST) & (lane < n_rest)
    b = jnp.sum(jnp.where(same, squares_rest, 0.0), 0, keepdims=True)
    row = iota((TAIL, n_main), 0)
    a_hi, b_hi = a.astype(BF16).astype(F32), b.astype(BF16).astype(F32)
    tail = jnp.where(row == 0, a_hi, jnp.where(row == 1, a - a_hi, 0.0))
    tail = jnp.where(row == 2, b_hi, jnp.where(row == 3, b - b_hi, tail))
    tail_ref[...] = tail.astype(BF16)


def partial_kernel(rows_ref, tail_ref, router_ref, own_ref, other_ref, out_ref):
    n = rows_ref.shape[0]
    for c, w_ref in enumerate((own_ref, other_ref)):
        out_ref[c * n : (c + 1) * n, :] = dot(rows_ref[...], w_ref[...]).astype(BF16)
    out_ref[2 * n : 2 * n + TAIL, :] = tail_ref[...]
    out_ref[2 * n + TAIL :, :] = router_ref[...]


def hidden_kernel(n_main, *refs):
    out_ref = refs[-1]
    units = out_ref.shape[1]
    n = (out_ref.shape[0] - 2 * TAIL) // 2

    def total(at, rows):
        parts = [r[at : at + rows, :].astype(F32) for r in refs[:-1]]
        return sum(parts[1:], parts[0])

    router = total(2 * n + TAIL, TAIL)
    router = router[:, :units] + router[:, units:]
    high = router.astype(BF16)
    out_ref[2 * n : 2 * n + TAIL, :] = high
    out_ref[2 * n + TAIL :, :] = (router - high.astype(F32)).astype(BF16)
    tail = total(2 * n, TAIL)
    mean_main = tail[0:1, :] + tail[1:2, :]
    mean_rest = (tail[2:3, :] + tail[3:4, :])[:, : n - n_main]

    def column(line):
        m = line.shape[1]
        return jnp.sum(jnp.where(iota((m, m), 0) == iota((m, m), 1), line, 0.0), 1, keepdims=True)

    squares = jnp.concatenate([column(mean_main), column(mean_rest)], 0)
    inverse = lax.rsqrt(squares / D + epsilon)
    for c in range(2):
        both = total(c * n, n)
        gate, upward = both[:, :units] * inverse, both[:, units:] * inverse
        out_ref[c * n : (c + 1) * n, :] = (jax.nn.silu(gate) * upward).astype(BF16)


def repeat_kernel(in_ref, out_ref):
    n = in_ref.shape[0] - 2 * TAIL
    for i in range(out_ref.shape[0] // n):
        out_ref[i * n : (i + 1) * n, :] = in_ref[:n, :]


def down_part(at_ref, dz, n, nx, nz, pieces, own_ref, other_ref):
    units = pieces[0].shape[1]
    side = (at_ref[1] + dz) % nz
    total = None
    for c, w_ref in enumerate((own_ref, other_ref)):
        for k in range(0, nx, 2):
            wide = jnp.concatenate([p[c * n : (c + 1) * n, :] for p in pieces[k : k + 2]], 1)
            blocks = [(at_ref[0] + nx - k - i) % nx * nz + side for i in range(2)]
            w = jnp.concatenate(
                [w_ref[pl.ds(pl.multiple_of(t * units, units), units), :] for t in blocks], 0
            )
            term = dot(wide, w)
            total = term if total is None else total + term
    return total


def down_first_kernel(homes, nx, nz, at_ref, own_ref, other_ref, *refs):
    pieces, out_ref, rest_ref = refs[:-2], refs[-2], refs[-1]
    units = pieces[0].shape[1]
    for c, w_ref in enumerate((own_ref, other_ref)):
        for x in range(nx):
            t = x * nz + (at_ref[1] + 1) % nz
            rest_ref[(c * nx + x) * units : (c * nx + x + 1) * units, :] = w_ref[
                pl.ds(pl.multiple_of(t * units, units), units), :
            ]
    out_ref[...] = down_part(at_ref, 0, homes * CAP, nx, nz, pieces, own_ref, other_ref)


def down_last_kernel(homes, nx, rest_ref, hid_ref, first_ref, out_ref, held_ref, sem):
    copy = pltpu.make_async_copy(first_ref, held_ref, sem)
    copy.start()
    width = first_ref.shape[1]
    half = width // 2
    n, n_main = homes * CAP, homes * MAIN
    depth = rest_ref.shape[0] // 2
    total = 0.0
    for c in range(2):
        starts = [(2 * x + c) * n for x in range(nx)]
        wide = jnp.concatenate([hid_ref[at : at + n, :] for at in starts], 1)
        total += dot(wide, rest_ref[c * depth : (c + 1) * depth, :])
    copy.wait()
    part = (total + held_ref[...]).astype(BF16)
    out_ref[:, :width] = part[:n_main]
    rest = part[n_main:]
    out_ref[:, width:] = (
        dot(rest_pick(homes, 0, True), rest[:, :half])
        + dot(rest_pick(homes, 1, True), rest[:, half:])
    ).astype(BF16)


def router_kernel(_, tok_ref, gain_ref, router_ref, *refs):
    out_ref = refs[4]
    values = tok_ref[...].astype(F32)
    count = values.shape[0]
    experts = router_ref.shape[0]
    sums = lax.dot_general(
        router_ref[...],
        values * gain_ref[...],
        (((1,), (1,)), ((), ())),
        precision=lax.Precision.HIGHEST,
        preferred_element_type=F32,
    )
    squares = jnp.sum(values * values, 1, keepdims=True)
    diagonal = iota((count, count), 0) == iota((count, count), 1)
    line = jnp.sum(jnp.where(diagonal, squares, 0.0), 0, keepdims=True)
    block = jnp.concatenate([sums, jnp.broadcast_to(line, (TAIL - experts, count))], 0)
    high = block.astype(BF16)
    low = (block - high.astype(F32)).astype(BF16)
    lanes = out_ref.shape[1] // 2
    blank = jnp.zeros((TAIL, lanes - count), BF16)
    out_ref[...] = jnp.concatenate([high, blank, low, blank], 1)


def join_kernel(in_ref, _, out_ref, __):
    out_ref[...] = in_ref[...]


def weights_kernel(experts, routes_ref, own_ref, other_ref, out_ref):
    count = routes_ref.shape[1]
    rows = out_ref.shape[0] // 2 // 3
    sums = jnp.zeros((TAIL, count), F32)
    for ref in (own_ref, other_ref):
        n = ref.shape[0]
        for at in (n - 2 * TAIL, n - TAIL):
            sums += ref[at : at + TAIL, :count].astype(F32)
    logits = sums[:experts] * lax.rsqrt(sums[experts : experts + 1] / D + epsilon)
    first, second = routes_ref[0:1, :], routes_ref[1:2, :]
    ids = iota((experts, count), 0)
    one = jnp.sum(jnp.where(ids == first, logits, 0.0), 0, keepdims=True)
    two = jnp.sum(jnp.where(ids == second, logits, 0.0), 0, keepdims=True)
    p_one, p_two = jax.nn.sigmoid(one - two), jax.nn.sigmoid(two - one)
    row = iota((rows, count), 0)
    expert = row // (rows // experts)
    named = ((first == expert) | (second == expert)).astype(F32)
    earlier = (iota((count, count), 0) < iota((count, count), 1)).astype(F32).astype(BF16)
    slot = dot(named.astype(BF16), earlier)
    weight = jnp.where(first == expert, p_one, 0.0) + jnp.where(second == expert, p_two, 0.0)
    place = row % MAIN
    main = jnp.where(slot == place.astype(F32), weight, 0.0)
    rest = jnp.where(slot == (MAIN + place % REST).astype(F32), weight, 0.0)
    blocks = [main, jnp.where(place < REST, rest, 0.0), jnp.where(place >= REST, rest, 0.0)]
    for i, block in enumerate(blocks):
        high = block.astype(BF16)
        low = (block - high.astype(F32)).astype(BF16)
        out_ref[i * rows : (i + 1) * rows, :] = high
        out_ref[(3 + i) * rows : (4 + i) * rows, :] = low


def combine_kernel(tok_ref, weight_ref, back_ref, out_ref):
    width = tok_ref.shape[1]
    half = width // 2
    rows = back_ref.shape[0]

    def mix(block, part):
        total = 0.0
        for i in (block, 3 + block):
            total += lax.dot_general(
                weight_ref[i * rows : (i + 1) * rows, :],
                part,
                (((0,), (0,)), ((), ())),
                preferred_element_type=F32,
            )
        return total

    total = tok_ref[...].astype(F32) + mix(0, back_ref[:, :width])
    rest = back_ref[:, width:]
    for h in range(2):
        cols = slice(h * half, (h + 1) * half)
        out_ref[:, cols] = (total[:, cols] + mix(1 + h, rest)).astype(BF16)


def shards(tokens, norm_gain, router_weight, routes, w_gate, w_up, w_down):
    experts = router_weight.shape[1]
    count, width = tokens.shape
    units = w_gate.shape[1]
    half = width // 2
    span = width + half
    nx, nz, ny = lax.axis_size("x"), lax.axis_size("zhi"), lax.axis_size("yl")
    x, zhi = lax.axis_index("x"), lax.axis_index("zhi")
    homes = experts * ny
    n = homes * CAP
    cols = 2 * units

    at = jnp.stack([x, zhi]).astype(jnp.int32)
    depth = nz * width
    piece = jax.ShapeDtypeStruct((depth, cols), BF16)

    def rows_for(k, *ws):
        start = ((x + k) % nx) * depth
        return jnp.concatenate([lax.dynamic_slice_in_dim(w, start, depth, 0) for w in ws], 1)

    w_x = {2: shift(rows_for(2, w_gate, w_up), "x", 2)}
    outgoing = local_kernel(
        functools.partial(pack_kernel, (nz, ny)),
        jax.ShapeDtypeStruct((nz * homes * MAIN, span + SIDE), BF16),
        routes.T,
        tokens,
        norm_gain[None, :],
    )
    outgoing, w_gate, w_up = lax.optimization_barrier((outgoing, w_gate, w_up))
    arrived = lax.all_to_all(
        outgoing.reshape(nz * homes, MAIN, span + SIDE), DISPATCH, 0, 0, tiled=True
    ).reshape(nz * homes * MAIN, span + SIDE)

    router, right, left, w_x[0] = local_kernel(
        router_kernel,
        [jax.ShapeDtypeStruct((TAIL, cols), BF16), piece, piece, piece],
        at,
        tokens,
        norm_gain[None, :],
        router_weight.T,
        outgoing,
        rows_for(1, w_gate, w_up),
        rows_for(3, w_gate, w_up),
        rows_for(0, w_gate, w_up),
        smem=1,
        far=4,
        far_outs=(1, 2, 3),
        aliases={5: 1, 6: 2, 7: 3},
        flops=WINDOW_FLOPS,
    )
    w_x[1], w_x[3] = shift(right, "x", 1), shift(left, "x", 3)
    router, w_x[2] = local_kernel(
        join_kernel,
        [jax.ShapeDtypeStruct((TAIL, cols), BF16), piece],
        router,
        w_x[2],
        far=1,
        far_outs=(1,),
        aliases={1: 1},
    )
    w_c = {k: shift(w_x[k], "core", 1) for k in (2, 0)}
    w_c[1], w_c[3] = shift(w_x[1], "core", 1), shift(w_x[3], "core", 1)
    rows, tail = local_kernel(
        functools.partial(unpack_kernel, homes, width),
        [
            jax.ShapeDtypeStruct((n, nz * width), BF16),
            jax.ShapeDtypeStruct((TAIL, homes * MAIN), BF16),
        ],
        arrived,
    )

    block = 2 * n + 2 * TAIL
    def partial(k):
        return local_kernel(
            partial_kernel,
            jax.ShapeDtypeStruct((block, cols), BF16),
            rows,
            tail,
            router,
            w_x[k],
            w_c[k],
            flops=4 * n * depth * cols,
        )

    mine = partial(0)
    got = [shift(partial(k), "x", -k) for k in (1, 3, 2)] + [mine]
    wd_other = shift(w_down, "core", 1)

    hidden = local_kernel(
        functools.partial(hidden_kernel, homes * MAIN),
        jax.ShapeDtypeStruct((block, units), BF16),
        *got,
    )

    hid_other = shift(hidden, "zhi", 1)
    own_rows = hidden[: 2 * n]
    other_rows = local_kernel(
        repeat_kernel, jax.ShapeDtypeStruct((nx * 2 * n, units), BF16), hid_other
    )
    other_rows = lax.all_to_all(
        other_rows.reshape(nx, 2 * n, units), "x", 0, 0, tiled=True
    ).reshape(nx * 2 * n, units)
    first, w_rest = local_kernel(
        functools.partial(down_first_kernel, homes, nx, nz),
        [
            jax.ShapeDtypeStruct((n, width), F32),
            jax.ShapeDtypeStruct((2 * nx * units, width), BF16),
        ],
        at,
        w_down,
        wd_other,
        *[shift(own_rows, "x", k) if k else own_rows for k in range(nx)],
        flops=FIRST_FLOPS,
        smem=1,
    )
    back = local_kernel(
        functools.partial(down_last_kernel, homes, nx),
        jax.ShapeDtypeStruct((homes * MAIN, span), BF16),
        w_rest,
        other_rows,
        first,
        far=1,
        scratch=[pltpu.VMEM((n, width), F32), pltpu.SemaphoreType.DMA],
        flops=2 * n * w_down.size,
    )
    back, routes = lax.optimization_barrier((back, routes))
    returned = lax.all_to_all(
        back.reshape(homes, MAIN, span), HOMES, 0, 0, tiled=True
    ).reshape(homes * MAIN, span)
    weights = local_kernel(
        functools.partial(weights_kernel, experts),
        jax.ShapeDtypeStruct((6 * homes * MAIN, count), BF16),
        routes.T,
        hidden,
        hid_other,
    )
    return local_kernel(
        combine_kernel,
        jax.ShapeDtypeStruct((count, width), BF16),
        tokens,
        weights,
        returned,
    )


def solution(mesh):
    fine = Mesh(mesh.devices.reshape(SIZES), NAMES)
    section, tp = NAMES[:4], NAMES[4:]
    placed = (
        P(section, tp),
        P(tp),
        P(tp, None),
        P(section, None),
        P(None, section + tp),
        P(None, section + tp),
        P(section, tp),
    )
    return jax.shard_map(
        shards, mesh=fine, in_specs=placed, out_specs=P(section, tp), check_vma=False
    )
```

```python
import functools

import jax
import jax.numpy as jnp
from jax import lax
from jax.experimental import pallas as pl
from jax.experimental.pallas import tpu as pltpu
from jax.sharding import Mesh, PartitionSpec as P

D = 6144
CAP = 12
MAIN = 8
REST = CAP - MAIN
SIDE = 128
TAIL = 16

epsilon = 1e-05

NAMES = ("zlo", "yh", "yl", "core", "x", "zhi")
SIZES = (4, 2, 4, 2, 4, 2)
HOMES = ("zlo", "yh", "yl")
DISPATCH = ("zhi", "zlo", "yh", "yl")
F32, BF16 = jnp.float32, jnp.bfloat16
VMEM_LIMIT = 16 * 1024 * 1024
WINDOW_FLOPS = 10**11
FIRST_FLOPS = 10**10


def shift(value, axis, by):
    size = lax.axis_size(axis)
    return lax.ppermute(value, axis, [(i, (i + by) % size) for i in range(size)])


def local_kernel(body, out, *args, flops=0, scratch=(), smem=0, far=0, far_outs=(), aliases=None):
    near = len(args) - smem - far
    spaces = [pltpu.SMEM] * smem + [pltpu.VMEM] * near + [pl.ANY] * far
    outs = out if isinstance(out, (list, tuple)) else [out]
    out_specs = [
        pl.BlockSpec(memory_space=pl.ANY if i in far_outs else pltpu.VMEM)
        for i in range(len(outs))
    ]
    moved = sum(a.size * a.dtype.itemsize for a in args) + sum(
        o.size * o.dtype.itemsize for o in outs
    )
    return pl.pallas_call(
        body,
        out_shape=out,
        in_specs=[pl.BlockSpec(memory_space=space) for space in spaces],
        scratch_shapes=list(scratch),
        out_specs=out_specs if isinstance(out, list) else out_specs[0],
        input_output_aliases=aliases or {},
        compiler_params=pltpu.CompilerParams(vmem_limit_bytes=VMEM_LIMIT),
        cost_estimate=pl.CostEstimate(flops=flops, bytes_accessed=moved, transcendentals=0),
    )(*args)


def iota(shape, dim):
    return lax.broadcasted_iota(jnp.int32, shape, dim)


def dot(a, b):
    return jnp.dot(a, b, preferred_element_type=F32)


def rest_pick(homes, half, wide):
    halves, plain = 2 * REST * homes, REST * homes
    shape = (halves, plain) if wide else (plain, halves)
    a, b = iota(shape, 0 if wide else 1), iota(shape, 1 if wide else 0)
    same = (a // (2 * REST) == b // REST) & (a % REST == b % REST)
    return (same & (a % (2 * REST) // REST == half)).astype(F32).astype(BF16)


def split(values):
    high = values.astype(BF16)
    return high, (values - high.astype(F32)).astype(BF16)


def pack_kernel(fan, routes_ref, tok_ref, gain_ref, out_ref):
    count, width = tok_ref.shape
    half = width // 2
    span = width + half
    first, second = routes_ref[0:1, :], routes_ref[1:2, :]
    experts = out_ref.shape[0] // (fan[0] * fan[1] * MAIN)
    n = experts * MAIN
    row = iota((n, count), 0)
    named = ((first == row // MAIN) | (second == row // MAIN)).astype(F32)
    earlier = (iota((count, count), 0) < iota((count, count), 1)).astype(F32).astype(BF16)
    slot = dot(named.astype(BF16), earlier)
    place = (row % MAIN).astype(F32)
    pick_main = jnp.where(slot == place, named, 0.0).astype(BF16)
    rest_place = (MAIN + row % REST).astype(F32)
    pick_rest = jnp.where(slot == rest_place, named, 0.0).astype(BF16)
    values = tok_ref[...].astype(F32)
    tok = (values * gain_ref[...]).astype(BF16)
    high, low = split(jnp.sum(values * values, 1, keepdims=True))
    lane = iota((count, SIDE), 1)
    zero = jnp.zeros((count, SIDE), F32)
    high, low = high.astype(F32) + zero, low.astype(F32) + zero
    side = 0.0
    for pick, at in ((pick_main, 0), (pick_rest, 2)):
        lanes = jnp.where(lane == at, high, jnp.where(lane == at + 1, low, 0.0))
        side += dot(pick, lanes.astype(BF16))
    main = dot(pick_main, tok).astype(BF16)
    rest = dot(pick_rest, tok)
    is_first = iota((n, half), 0) % MAIN < REST
    rest = jnp.where(is_first, rest[:, :half], rest[:, half:]).astype(BF16)
    side = side.astype(BF16)
    for e in range(experts):
        block = slice(e * MAIN, (e + 1) * MAIN)
        parts = [jnp.concatenate([p[block]] * fan[1], 0) for p in (main, rest, side)]
        for z in range(fan[0]):
            at = pl.ds((z * experts + e) * fan[1] * MAIN, fan[1] * MAIN)
            out_ref[at, :width] = parts[0]
            out_ref[at, width:span] = parts[1]
            out_ref[at, span:] = parts[2]


def unpack_kernel(homes, width, in_ref, rows_ref, tail_ref):
    half = width // 2
    span = width + half
    n_main, n_rest = homes * MAIN, homes * REST
    squares = jnp.zeros((n_main, SIDE), F32)
    picks = [rest_pick(homes, h, False) for h in range(2)]
    for z in range(2):
        block = pl.ds(z * n_main, n_main)
        rows_ref[:n_main, z * width : (z + 1) * width] = in_ref[block, :width]
        halves = in_ref[block, width:span]
        for h in range(2):
            at = slice(z * width + h * half, z * width + (h + 1) * half)
            rows_ref[n_main:, at] = dot(picks[h], halves).astype(BF16)
        squares += in_ref[block, span:].astype(F32)
    squares_main = squares[:, 0:1] + squares[:, 1:2]
    of_first = (iota((n_main, 1), 0) % MAIN < REST).astype(F32)
    squares_rest = (squares[:, 2:3] + squares[:, 3:4]) * of_first

    def lanes(column):
        n = column.shape[0]
        return jnp.sum(jnp.where(iota((n, n), 0) == iota((n, n), 1), column, 0.0), 0, keepdims=True)

    a = lanes(squares_main)
    source, lane = iota((n_main, n_main), 0), iota((n_main, n_main), 1)
    same = (source // MAIN == lane // REST) & (source % MAIN == lane % REST) & (lane < n_rest)
    b = jnp.sum(jnp.where(same, squares_rest, 0.0), 0, keepdims=True)
    row = iota((TAIL, n_main), 0)
    a_hi, b_hi = a.astype(BF16).astype(F32), b.astype(BF16).astype(F32)
    tail = jnp.where(row == 0, a_hi, jnp.where(row == 1, a - a_hi, 0.0))
    tail = jnp.where(row == 2, b_hi, jnp.where(row == 3, b - b_hi, tail))
    tail_ref[...] = tail.astype(BF16)


def partial_kernel(rows_ref, tail_ref, router_ref, own_ref, other_ref, out_ref):
    n = rows_ref.shape[0]
    for c, w_ref in enumerate((own_ref, other_ref)):
        out_ref[c * n : (c + 1) * n, :] = dot(rows_ref[...], w_ref[...]).astype(BF16)
    out_ref[2 * n : 2 * n + TAIL, :] = tail_ref[...]
    out_ref[2 * n + TAIL :, :] = router_ref[...]


def hidden_kernel(n_main, *refs):
    out_ref = refs[-1]
    units = out_ref.shape[1]
    n = (out_ref.shape[0] - 2 * TAIL) // 2

    def total(at, rows):
        parts = [r[at : at + rows, :].astype(F32) for r in refs[:-1]]
        return sum(parts[1:], parts[0])

    router = total(2 * n + TAIL, TAIL)
    router = router[:, :units] + router[:, units:]
    high = router.astype(BF16)
    out_ref[2 * n : 2 * n + TAIL, :] = high
    out_ref[2 * n + TAIL :, :] = (router - high.astype(F32)).astype(BF16)
    tail = total(2 * n, TAIL)
    mean_main = tail[0:1, :] + tail[1:2, :]
    mean_rest = (tail[2:3, :] + tail[3:4, :])[:, : n - n_main]

    def column(line):
        m = line.shape[1]
        return jnp.sum(jnp.where(iota((m, m), 0) == iota((m, m), 1), line, 0.0), 1, keepdims=True)

    squares = jnp.concatenate([column(mean_main), column(mean_rest)], 0)
    inverse = lax.rsqrt(squares / D + epsilon)
    for c in range(2):
        both = total(c * n, n)
        gate, upward = both[:, :units] * inverse, both[:, units:] * inverse
        out_ref[c * n : (c + 1) * n, :] = (jax.nn.silu(gate) * upward).astype(BF16)


def repeat_kernel(in_ref, out_ref):
    n = in_ref.shape[0] - 2 * TAIL
    for i in range(out_ref.shape[0] // n):
        out_ref[i * n : (i + 1) * n, :] = in_ref[:n, :]


def down_part(at_ref, dz, n, nx, nz, pieces, own_ref, other_ref):
    units = pieces[0].shape[1]
    side = (at_ref[1] + dz) % nz
    total = None
    for c, w_ref in enumerate((own_ref, other_ref)):
        for k in range(0, nx, 2):
            wide = jnp.concatenate([p[c * n : (c + 1) * n, :] for p in pieces[k : k + 2]], 1)
            blocks = [(at_ref[0] + nx - k - i) % nx * nz + side for i in range(2)]
            w = jnp.concatenate(
                [w_ref[pl.ds(pl.multiple_of(t * units, units), units), :] for t in blocks], 0
            )
            term = dot(wide, w)
            total = term if total is None else total + term
    return total


def down_first_kernel(homes, nx, nz, at_ref, own_ref, other_ref, *refs):
    pieces, out_ref, rest_ref = refs[:-2], refs[-2], refs[-1]
    units = pieces[0].shape[1]
    for c, w_ref in enumerate((own_ref, other_ref)):
        for x in range(nx):
            t = x * nz + (at_ref[1] + 1) % nz
            rest_ref[(c * nx + x) * units : (c * nx + x + 1) * units, :] = w_ref[
                pl.ds(pl.multiple_of(t * units, units), units), :
            ]
    total = down_part(at_ref, 0, homes * CAP, nx, nz, pieces, own_ref, other_ref)
    out_ref[...] = total.astype(BF16)


def down_last_kernel(homes, nx, first_ref, rest_ref, hid_ref, out_ref):
    width = first_ref.shape[1]
    half = width // 2
    n, n_main = homes * CAP, homes * MAIN
    depth = rest_ref.shape[0] // 2
    total = first_ref[...].astype(F32)
    for c in range(2):
        starts = [(2 * x + c) * n for x in range(nx)]
        wide = jnp.concatenate([hid_ref[at : at + n, :] for at in starts], 1)
        total += dot(wide, rest_ref[c * depth : (c + 1) * depth, :])
    part = total.astype(BF16)
    out_ref[:, :width] = part[:n_main]
    rest = part[n_main:]
    out_ref[:, width:] = (
        dot(rest_pick(homes, 0, True), rest[:, :half])
        + dot(rest_pick(homes, 1, True), rest[:, half:])
    ).astype(BF16)


def router_kernel(_, tok_ref, gain_ref, router_ref, *refs):
    out_ref = refs[4]
    values = tok_ref[...].astype(F32)
    count = values.shape[0]
    experts = router_ref.shape[0]
    sums = lax.dot_general(
        router_ref[...],
        values * gain_ref[...],
        (((1,), (1,)), ((), ())),
        precision=lax.Precision.HIGHEST,
        preferred_element_type=F32,
    )
    squares = jnp.sum(values * values, 1, keepdims=True)
    diagonal = iota((count, count), 0) == iota((count, count), 1)
    line = jnp.sum(jnp.where(diagonal, squares, 0.0), 0, keepdims=True)
    block = jnp.concatenate([sums, jnp.broadcast_to(line, (TAIL - experts, count))], 0)
    high = block.astype(BF16)
    low = (block - high.astype(F32)).astype(BF16)
    lanes = out_ref.shape[1] // 2
    blank = jnp.zeros((TAIL, lanes - count), BF16)
    out_ref[...] = jnp.concatenate([high, blank, low, blank], 1)


def join_kernel(in_ref, _, out_ref, __):
    out_ref[...] = in_ref[...]


def weights_kernel(experts, routes_ref, own_ref, other_ref, out_ref):
    count = routes_ref.shape[1]
    rows = out_ref.shape[0] // 2 // 3
    sums = jnp.zeros((TAIL, count), F32)
    for ref in (own_ref, other_ref):
        n = ref.shape[0]
        for at in (n - 2 * TAIL, n - TAIL):
            sums += ref[at : at + TAIL, :count].astype(F32)
    logits = sums[:experts] * lax.rsqrt(sums[experts : experts + 1] / D + epsilon)
    first, second = routes_ref[0:1, :], routes_ref[1:2, :]
    ids = iota((experts, count), 0)
    one = jnp.sum(jnp.where(ids == first, logits, 0.0), 0, keepdims=True)
    two = jnp.sum(jnp.where(ids == second, logits, 0.0), 0, keepdims=True)
    p_one, p_two = jax.nn.sigmoid(one - two), jax.nn.sigmoid(two - one)
    row = iota((rows, count), 0)
    expert = row // (rows // experts)
    named = ((first == expert) | (second == expert)).astype(F32)
    earlier = (iota((count, count), 0) < iota((count, count), 1)).astype(F32).astype(BF16)
    slot = dot(named.astype(BF16), earlier)
    weight = jnp.where(first == expert, p_one, 0.0) + jnp.where(second == expert, p_two, 0.0)
    place = row % MAIN
    main = jnp.where(slot == place.astype(F32), weight, 0.0)
    rest = jnp.where(slot == (MAIN + place % REST).astype(F32), weight, 0.0)
    blocks = [main, jnp.where(place < REST, rest, 0.0), jnp.where(place >= REST, rest, 0.0)]
    for i, block in enumerate(blocks):
        high = block.astype(BF16)
        low = (block - high.astype(F32)).astype(BF16)
        out_ref[i * rows : (i + 1) * rows, :] = high
        out_ref[(3 + i) * rows : (4 + i) * rows, :] = low


def combine_kernel(tok_ref, weight_ref, back_ref, out_ref):
    width = tok_ref.shape[1]
    half = width // 2
    rows = back_ref.shape[0]

    def mix(block, part):
        total = 0.0
        for i in (block, 3 + block):
            total += lax.dot_general(
                weight_ref[i * rows : (i + 1) * rows, :],
                part,
                (((0,), (0,)), ((), ())),
                preferred_element_type=F32,
            )
        return total

    total = tok_ref[...].astype(F32) + mix(0, back_ref[:, :width])
    rest = back_ref[:, width:]
    for h in range(2):
        cols = slice(h * half, (h + 1) * half)
        out_ref[:, cols] = (total[:, cols] + mix(1 + h, rest)).astype(BF16)


def shards(tokens, norm_gain, router_weight, routes, w_gate, w_up, w_down):
    experts = router_weight.shape[1]
    count, width = tokens.shape
    units = w_gate.shape[1]
    half = width // 2
    span = width + half
    nx, nz, ny = lax.axis_size("x"), lax.axis_size("zhi"), lax.axis_size("yl")
    x, zhi = lax.axis_index("x"), lax.axis_index("zhi")
    homes = experts * ny
    n = homes * CAP
    cols = 2 * units

    at = jnp.stack([x, zhi]).astype(jnp.int32)
    depth = nz * width
    piece = jax.ShapeDtypeStruct((depth, cols), BF16)

    def rows_for(k, *ws):
        start = ((x + k) % nx) * depth
        return jnp.concatenate([lax.dynamic_slice_in_dim(w, start, depth, 0) for w in ws], 1)

    w_x = {2: shift(rows_for(2, w_gate, w_up), "x", 2)}
    outgoing = local_kernel(
        functools.partial(pack_kernel, (nz, ny)),
        jax.ShapeDtypeStruct((nz * homes * MAIN, span + SIDE), BF16),
        routes.T,
        tokens,
        norm_gain[None, :],
    )
    outgoing, w_gate, w_up = lax.optimization_barrier((outgoing, w_gate, w_up))
    arrived = lax.all_to_all(
        outgoing.reshape(nz * homes, MAIN, span + SIDE), DISPATCH, 0, 0, tiled=True
    ).reshape(nz * homes * MAIN, span + SIDE)

    router, right, left, w_x[0] = local_kernel(
        router_kernel,
        [jax.ShapeDtypeStruct((TAIL, cols), BF16), piece, piece, piece],
        at,
        tokens,
        norm_gain[None, :],
        router_weight.T,
        outgoing,
        rows_for(1, w_gate, w_up),
        rows_for(3, w_gate, w_up),
        rows_for(0, w_gate, w_up),
        smem=1,
        far=4,
        far_outs=(1, 2, 3),
        aliases={5: 1, 6: 2, 7: 3},
        flops=WINDOW_FLOPS,
    )
    w_x[1], w_x[3] = shift(right, "x", 1), shift(left, "x", 3)
    router, w_x[2] = local_kernel(
        join_kernel,
        [jax.ShapeDtypeStruct((TAIL, cols), BF16), piece],
        router,
        w_x[2],
        far=1,
        far_outs=(1,),
        aliases={1: 1},
    )
    w_c = {k: shift(w_x[k], "core", 1) for k in (2, 0)}
    w_c[1], w_c[3] = shift(w_x[1], "core", 1), shift(w_x[3], "core", 1)
    rows, tail = local_kernel(
        functools.partial(unpack_kernel, homes, width),
        [
            jax.ShapeDtypeStruct((n, nz * width), BF16),
            jax.ShapeDtypeStruct((TAIL, homes * MAIN), BF16),
        ],
        arrived,
    )

    block = 2 * n + 2 * TAIL
    def partial(k):
        return local_kernel(
            partial_kernel,
            jax.ShapeDtypeStruct((block, cols), BF16),
            rows,
            tail,
            router,
            w_x[k],
            w_c[k],
            flops=4 * n * depth * cols,
        )

    mine = partial(0)
    got = [shift(partial(k), "x", -k) for k in (1, 3, 2)] + [mine]
    wd_other = shift(w_down, "core", 1)

    hidden = local_kernel(
        functools.partial(hidden_kernel, homes * MAIN),
        jax.ShapeDtypeStruct((block, units), BF16),
        *got,
    )

    hid_other = shift(hidden, "zhi", 1)
    own_rows = hidden[: 2 * n]
    other_rows = local_kernel(
        repeat_kernel, jax.ShapeDtypeStruct((nx * 2 * n, units), BF16), hid_other
    )
    other_rows = lax.all_to_all(
        other_rows.reshape(nx, 2 * n, units), "x", 0, 0, tiled=True
    ).reshape(nx * 2 * n, units)
    first, w_rest = local_kernel(
        functools.partial(down_first_kernel, homes, nx, nz),
        [
            jax.ShapeDtypeStruct((n, width), BF16),
            jax.ShapeDtypeStruct((2 * nx * units, width), BF16),
        ],
        at,
        w_down,
        wd_other,
        *[shift(own_rows, "x", k) if k else own_rows for k in range(nx)],
        flops=FIRST_FLOPS,
        smem=1,
    )
    back = local_kernel(
        functools.partial(down_last_kernel, homes, nx),
        jax.ShapeDtypeStruct((homes * MAIN, span), BF16),
        first,
        w_rest,
        other_rows,
        flops=2 * n * w_down.size,
    )
    back, routes = lax.optimization_barrier((back, routes))
    returned = lax.all_to_all(
        back.reshape(homes, MAIN, span), HOMES, 0, 0, tiled=True
    ).reshape(homes * MAIN, span)
    weights = local_kernel(
        functools.partial(weights_kernel, experts),
        jax.ShapeDtypeStruct((6 * homes * MAIN, count), BF16),
        routes.T,
        hidden,
        hid_other,
    )
    return local_kernel(
        combine_kernel,
        jax.ShapeDtypeStruct((count, width), BF16),
        tokens,
        weights,
        returned,
    )


def solution(mesh):
    fine = Mesh(mesh.devices.reshape(SIZES), NAMES)
    section, tp = NAMES[:4], NAMES[4:]
    placed = (
        P(section, tp),
        P(tp),
        P(tp, None),
        P(section, None),
        P(None, section + tp),
        P(None, section + tp),
        P(section, tp),
    )
    return jax.shard_map(
        shards, mesh=fine, in_specs=placed, out_specs=P(section, tp), check_vma=False
    )
```
